256 devices in a mesh: dp: 32 (over x, y, core), vocab: 8 (over z).
Axes of the slice: x: 4, y: 4, z: 8, core: 2. Of those that a mesh axis runs over, the one named last changes fastest.
Arguments:
- encoder_proj: bfloat16 [6144, 512], P('dp'), may hold values from -4 to 4
- predictor_proj: bfloat16 [128, 64, 512], P('dp'), may hold values from -5 to 5
- out_weight: bfloat16 [512, 30720], P(None, 'vocab'), may hold values from -1 to 1
- frame_utt: int32 [6144], P('dp'), may hold values from 0 to 127, as said below
- prune_start: int32 [6144], P('dp'), may hold values from 0 to 59, as said below
- labels: int32 [6144, 5], P('dp'), may hold values from 1 to 30719
- utt_len: int32 [128], replicated, may hold values from 5 to 63
- blank_occ: float32 [6144, 5], P('dp'), may hold values from 0.05 to 1
- label_occ: float32 [6144, 5], P('dp'), may hold values from 0.05 to 1
- frame_weight: float32 [6144], P('dp'), may hold values from 0.25 to 1
Outputs:
- grad_weight: float32 [512, 30720], P('dp', 'vocab')
- grad_encoder: float32 [6144, 512], P('dp', 'vocab')
- grad_predictor: float32 [128, 64, 512], P('dp', None, 'vocab')
The draws below stay inside these ranges and needn't reach their ends.
Inputs may be any that keep to these rules, and one draw needn't show every extreme that they name: `frame_utt`: frames are in utterance order; the utterances of index d of dp are d * 4 to (d + 1) * 4 - 1, and each frame belongs to an utterance of its own index of dp or of the index before. prune_start[t] + 4 is at most utt_len[frame_utt[t]].
All inputs are finite; a program needn't handle non-finite values.
Results may differ from the reference program's by a relative error of at most 0.0043.
Values may be sent and summed in bfloat16 or wider, within the bound.
A program may use at most 64 MiB of HBM per device.

```python
import math
import jax
import jax.numpy as jnp
from jax import lax

J = 512
V = 30720
S = 5
P_SIZE = 64
UTT_DEV = 4
TDEV = 192
FRAMES = 6144
UTTS = 128


def utterance_layout(key):
    devices = FRAMES // TDEV
    key_len, key_cut, key_share = jax.random.split(jax.random.fold_in(key, 101), 3)
    lengths = jax.random.randint(key_len, (UTTS,), S, P_SIZE).astype(jnp.int32)
    lengths = lengths.at[0].set(P_SIZE - 1)
    cuts = jax.random.randint(key_cut, (devices,), 1, TDEV // 2 + 1).astype(jnp.int32)
    cuts = cuts.at[0].set(0)
    shares = jax.random.randint(key_share, (devices, UTT_DEV), 1, 5).astype(jnp.int32)
    spare = TDEV - cuts - UTT_DEV
    pieces = 1 + spare[:, None] * shares // jnp.sum(shares, axis=1, keepdims=True)
    ends = jnp.cumsum(pieces, axis=1)[:, :UTT_DEV - 1]
    local = jnp.arange(TDEV, dtype=jnp.int32)[None, :] - cuts[:, None]
    within = jnp.sum((local[:, :, None] >= ends[:, None, :]).astype(jnp.int32), axis=2)
    owner = jnp.arange(devices, dtype=jnp.int32)[:, None] * UTT_DEV
    mapping = jnp.where(local < 0, owner - 1, owner + within).reshape(FRAMES)
    return (lengths, mapping.astype(jnp.int32))


def draw_utt_len(key, part):
    lengths, mapping = utterance_layout(key)
    return lengths


def draw_frame_utt(key, part):
    lengths, mapping = utterance_layout(key)
    return mapping


def draw_prune_start(key, part):
    lengths, mapping = utterance_layout(key)
    key = jax.random.fold_in(key, 3)
    span = lengths[mapping] - S + 2
    raw = jax.random.randint(key, (FRAMES,), 0, 1 << 20).astype(jnp.int32)
    starts = raw % span
    starts = starts.at[0].set(P_SIZE - S)
    return starts.astype(jnp.int32)


def draw_encoder_proj(key, part):
    key = jax.random.fold_in(key, 5)
    base = jnp.clip(jax.random.normal(key, (FRAMES, J), jnp.float32), -4.0, 4.0)
    values = base
    return values.astype(jnp.bfloat16)


def block_loudness(key, spread):
    cols = jnp.arange(V, dtype=jnp.int32)
    owners = cols * 8 // V
    levels = jnp.exp(jax.random.uniform(key, (8,), jnp.float32, -spread, spread))
    picks = owners[:, None] == jnp.arange(8, dtype=jnp.int32)[None, :]
    return jnp.sum(jnp.where(picks, levels[None, :], 0.0), axis=1)


def draw_out_weight(key, part):
    key = jax.random.fold_in(key, 7)
    key_base, key_loud = jax.random.split(key, 2)
    drawn = jnp.clip(jax.random.normal(key_base, (J, V), jnp.float32), -3.0, 3.0) / math.sqrt(J)
    loudness = 2.5 * block_loudness(key_loud, 0.35)
    values = drawn * loudness[None, :]
    limit = 1.0 + 256 // J
    return jnp.clip(values, -limit, limit).astype(jnp.bfloat16)


def touch_ends(values, key, smallest, high):
    spot = [jax.random.randint(jax.random.fold_in(key, axis), (), 0, length) for axis, length in enumerate(values.shape)]
    widest = values.shape.index(max(values.shape))
    beside = spot[:widest] + [(spot[widest] + 1) % values.shape[widest]] + spot[widest + 1:]
    return values.at[tuple(spot)].set(smallest).at[tuple(beside)].set(high)


def level_of(own_key, dims, shards, least, largest):
    level, own = 1.0, jax.random.fold_in(own_key, 6)
    for dim, blocks in shards:
        steps = jnp.exp(jax.random.uniform(jax.random.fold_in(own, dim), (blocks,), jnp.float32, least / len(shards), largest / len(shards)))
        level = level * jnp.repeat(steps, dims[dim] // blocks).reshape([-1 if axis == dim else 1 for axis in range(len(dims))])
    return level


def gaussian(own_key, dims, deviation, bound, shards=(), held_as=jnp.bfloat16):
    level = level_of(own_key, dims, shards, -0.22, 0.18) if shards else 1.0
    values = jax.random.normal(own_key, dims, jnp.float32) * deviation * level
    return jnp.minimum(jnp.maximum(values, -bound), bound).astype(held_as)


def setup_inputs(seed: int = 0) -> dict:
    streams_of = jax.random.split(jax.random.key(seed), 11)
    encoder_proj = draw_encoder_proj(jax.random.fold_in(streams_of[10], 71), 0)
    predictor_proj = gaussian(streams_of[1], (UTTS, P_SIZE, J), 1.0, 5.0, ((0, 32),))
    out_weight = draw_out_weight(jax.random.fold_in(streams_of[10], 71), 0)
    frame_utt = draw_frame_utt(jax.random.fold_in(streams_of[10], 71), 0)
    prune_start = draw_prune_start(jax.random.fold_in(streams_of[10], 71), 0)
    labels = touch_ends(jax.random.randint(streams_of[5], (FRAMES, S), 1, V), jax.random.fold_in(streams_of[5], 1), 1, V - 1).astype(jnp.int32)
    utt_len = draw_utt_len(jax.random.fold_in(streams_of[10], 71), 0)
    blank_occ = jnp.clip(jnp.exp(math.log(1.0) - 2.9957323 * jax.random.uniform(streams_of[7], (FRAMES, S), jnp.float32) ** level_of(streams_of[7], (FRAMES, S), ((0, 32),), -0.2, 0.2)), 0.05, 1.0)
    label_occ = jnp.clip(jnp.exp(math.log(1.0) - 2.9957323 * jax.random.uniform(streams_of[8], (FRAMES, S), jnp.float32) ** level_of(streams_of[8], (FRAMES, S), ((0, 32),), -0.2, 0.2)), 0.05, 1.0)
    frame_weight = jnp.clip(jnp.exp(math.log(1.0) - 1.3862944 * jax.random.uniform(streams_of[9], (FRAMES,), jnp.float32) ** level_of(streams_of[9], (FRAMES,), ((0, 32),), -0.2, 0.2)), 0.25, 1.0)
    return {"encoder_proj": encoder_proj, "predictor_proj": predictor_proj, "out_weight": out_weight, "frame_utt": frame_utt, "prune_start": prune_start, "labels": labels, "utt_len": utt_len, "blank_occ": blank_occ, "label_occ": label_occ, "frame_weight": frame_weight}


def reference(encoder_proj, predictor_proj, out_weight, frame_utt, prune_start, labels, utt_len, blank_occ, label_occ, frame_weight):
    offsets = jnp.arange(S, dtype=jnp.int32)
    positions = (prune_start[:, None] + offsets[None, :]).astype(jnp.int32)
    limits = utt_len[frame_utt]
    validity = (positions < limits[:, None]).astype(jnp.float32)
    blank_coef = frame_weight[:, None] * blank_occ
    label_coef = frame_weight[:, None] * label_occ * validity
    gathered = predictor_proj[frame_utt[:, None], positions]
    blocks = FRAMES // TDEV
    columns = jnp.arange(V, dtype=jnp.int32)

    def one_block(carry, inputs):
        enc_block, pred_block, label_ids, blank_block, label_block = inputs
        summed = enc_block[:, None, :].astype(jnp.float32) + pred_block.astype(jnp.float32)
        joint_act = jnp.tanh(summed).reshape(TDEV * S, J)
        joint_low = joint_act.astype(jnp.bfloat16)
        logits = jnp.dot(joint_low, out_weight, preferred_element_type=jnp.float32)
        peak = jnp.max(logits, axis=1, keepdims=True)
        expon = jnp.exp(logits - peak)
        total = jnp.sum(expon, axis=1, keepdims=True)
        blank_flat = blank_block.reshape(TDEV * S, 1)
        label_flat = label_block.reshape(TDEV * S, 1)
        ids_flat = label_ids.reshape(TDEV * S, 1)
        is_blank = (columns[None, :] == 0).astype(jnp.float32)
        is_label = (columns[None, :] == ids_flat).astype(jnp.float32)
        logit_grad = (blank_flat + label_flat) * (expon / total) - blank_flat * is_blank - label_flat * is_label
        grad_low = logit_grad.astype(jnp.bfloat16)
        hidden_grad = lax.dot_general(grad_low, out_weight, (((1,), (1,)), ((), ())), preferred_element_type=jnp.float32)
        act_grad = hidden_grad * (1.0 - joint_act * joint_act)
        carry = carry + lax.dot_general(joint_low, grad_low, (((0,), (0,)), ((), ())), preferred_element_type=jnp.float32)
        return carry, act_grad.reshape(TDEV, S, J)

    start = jnp.zeros((J, V), jnp.float32)
    grad_weight, act_blocks = lax.scan(one_block, start, (
        encoder_proj.reshape(blocks, TDEV, J),
        gathered.reshape(blocks, TDEV, S, J),
        labels.reshape(blocks, TDEV, S),
        blank_coef.reshape(blocks, TDEV, S),
        label_coef.reshape(blocks, TDEV, S)))
    act_grads = act_blocks.reshape(FRAMES, S, J)
    grad_encoder = jnp.sum(act_grads, axis=1)
    grad_predictor = jnp.zeros((UTTS, P_SIZE, J), jnp.float32).at[frame_utt[:, None], positions].add(act_grads)
    return grad_weight, grad_encoder, grad_predictor
```

```python
import functools

import jax
import jax.numpy as jnp
from jax import lax
from jax.experimental import pallas as pl
from jax.experimental.pallas import tpu as pltpu
from jax.sharding import PartitionSpec as P

MESH = pl.DeviceIdType.MESH
F32 = jnp.float32
BF16 = jnp.bfloat16
KEPT = 5
HALF = 512
WCOLS = 768
LANES = 128


def iota(shape, dim):
    return lax.broadcasted_iota(jnp.int32, shape, dim)


def kernel(
    grid,
    enc_hbm,
    pred_hbm,
    w_hbm,
    futt_hbm,
    pstart_hbm,
    labels_hbm,
    ulen_hbm,
    bocc_hbm,
    locc_hbm,
    fw_hbm,
    gw_ref,
    ge_ref,
    gp_ref,
    enc,
    table,
    w,
    futt,
    pstart,
    labels,
    ulen,
    bocc,
    locc,
    fw,
    aux,
    auxt,
    labrep,
    lrep,
    bl0,
    coef,
    frep,
    picker,
    act32,
    actb,
    actt,
    actp,
    ebuf,
    mx,
    stat,
    ssend,
    srecv,
    scol,
    gbuf,
    hsend,
    hrecv,
    agrad,
    pbuf,
    csend,
    crecv,
    wsum,
    xr1,
    yst,
    yst32,
    yr2,
    yr1,
    xst,
    xst32,
    xr2,
    gpsend,
    gprecv,
    local_sem,
    pred_sem,
    stat_ssem,
    stat_rsem,
    h_ssem,
    h_rsem,
    c_ssem,
    c_rsem,
    p1_ssem,
    p1_rsem,
    p2_ssem,
    p2_rsem,
    gp_sem,
):
    nx, ny, nz = grid
    ndp = nx * ny * 2
    frames = enc.shape[0]
    rows = frames * KEPT
    width, vlocal = w.shape
    own_rows = pred_hbm.shape[0]
    dp = lax.axis_index("dp")
    z = lax.axis_index("vocab")
    cx = dp // (2 * ny)
    cy = lax.rem(dp // 2, ny)
    core = lax.rem(dp, 2)
    wx = nx - 1
    wy = ny - 1

    def zpeer(i):
        return (dp, lax.rem(z + i, nz))

    def xpeer(i):
        return ((lax.rem(cx + i, nx) * ny + cy) * 2 + core, z)

    def ypeer(i):
        return ((cx * ny + lax.rem(cy + i, ny)) * 2 + core, z)

    partner = (dp + 1 - 2 * core, z)
    following = (lax.rem(dp + 1, ndp), z)
    before = (lax.rem(dp + ndp - 1, ndp), z)

    loads = []
    for i, (src, dst) in enumerate(
        (
            (futt_hbm, futt),
            (pstart_hbm, pstart),
            (labels_hbm, labels),
            (ulen_hbm, ulen),
            (bocc_hbm, bocc),
            (locc_hbm, locc),
            (fw_hbm, fw),
            (enc_hbm, enc),
            (pred_hbm, table.at[pl.ds(own_rows, own_rows)]),
            (w_hbm, w),
        )
    ):
        cp = pltpu.make_async_copy(src, dst, local_sem.at[i])
        cp.start()
        loads.append(cp)

    barrier = pltpu.get_barrier_semaphore()
    peers = [zpeer(i) for i in range(1, nz)] + [xpeer(i) for i in range(1, nx)]
    peers += [ypeer(i) for i in range(1, ny)] + [partner, following, before]
    for peer in peers:
        pl.semaphore_signal(barrier, inc=1, device_id=peer, device_id_type=MESH)

    def remote(src, dst, ssem, rsem, peer):
        return pltpu.make_async_remote_copy(
            src_ref=src, dst_ref=dst, send_sem=ssem, recv_sem=rsem, device_id=peer, device_id_type=MESH
        )

    aux[...] = jnp.zeros_like(aux)
    tail = act32.shape[0] - rows
    act32[pl.ds(rows, tail), :] = jnp.zeros((tail, width), F32)
    gbuf[pl.ds(rows, tail), :] = jnp.zeros((tail, vlocal), BF16)
    picker[pl.ds(rows, tail), :] = jnp.zeros((tail, 2 * own_rows), BF16)
    stat[...] = jnp.zeros_like(stat)
    scol[...] = jnp.zeros_like(scol)
    pl.semaphore_wait(barrier, len(peers))
    pred_copy = remote(
        pred_hbm, table.at[pl.ds(0, own_rows)], pred_sem.at[0], pred_sem.at[1], following
    )
    pred_copy.start()

    for cp in loads[:8]:
        cp.wait()
    aux[0:1, 0:frames] = ((futt[...] - (dp - 1) * (own_rows // 64)) * 64 + pstart[...]).astype(F32)
    aux[1:2, 0:frames] = futt[...].astype(F32)
    aux[2:3, 0:frames] = pstart[...].astype(F32)
    aux[8 : 8 + KEPT, 0:frames] = labels[...].astype(F32)
    aux[16 : 16 + KEPT, 0:frames] = fw[...] * bocc[...]
    aux[24 : 24 + KEPT, 0:frames] = fw[...] * locc[...]
    auxt[...] = aux[...].T

    def column(i):
        return auxt[0:frames, i : i + 1]

    utts = ulen.shape[1]
    futt_col = column(1).astype(jnp.int32)
    found = futt_col == iota((frames, utts), 1)
    limit = jnp.sum(jnp.where(found, ulen[...].astype(F32), 0.0), axis=1, keepdims=True)
    start_col = column(2)
    base_col = column(0).astype(jnp.int32)
    lane = iota((frames, LANES), 1)
    first = jnp.logical_and(lane == 0, z == 0)
    table_iota = iota((frames, 2 * own_rows), 1)
    for k in range(KEPT):
        at = pl.ds(k * frames, frames)
        valid = (start_col + float(k) < limit).astype(F32)
        label_coef = column(24 + k) * valid
        blank_coef = column(16 + k)
        labrep[at, :] = jnp.broadcast_to(column(8 + k).astype(jnp.int32) - z * vlocal, (frames, LANES))
        lrep[at, :] = jnp.broadcast_to(label_coef, (frames, LANES))
        bl0[at, :] = jnp.where(first, jnp.broadcast_to(blank_coef, (frames, LANES)), 0.0)
        coef[at, :] = jnp.broadcast_to(blank_coef + label_coef, (frames, LANES))
        picker[at, :] = (base_col + k == table_iota).astype(BF16)

    loads[8].wait()
    pred_copy.wait()
    for k in range(KEPT):
        at = pl.ds(k * frames, frames)
        picked = jnp.dot(picker[at, :], table[...], preferred_element_type=F32)
        act = jnp.tanh(enc[...].astype(F32) + picked)
        act32[at, :] = act
        actb[at, :] = act.astype(BF16)
    share = width // ndp
    for i in range(act32.shape[0] // LANES):
        cols = pl.ds(i * LANES, LANES)
        turned = act32[cols, :].T
        actt[:, cols] = turned
        split = turned.reshape(nx * ny, 2, share, LANES)
        for c in range(2):
            actp[pl.ds(c * (width // 2), width // 2), cols] = (
                split[:, c].reshape(width // 2, LANES).astype(BF16)
            )

    loads[9].wait()

    stat_copies = []
    for h in range(2):
        r0 = h * HALF
        count = min(HALF, rows - r0)
        mx[...] = jnp.full(mx.shape, -jnp.inf, F32)

        def logits_step(c, carry, r0=r0, count=count):
            cols = pl.ds(pl.multiple_of(c * 256, 256), 256)
            block = jnp.dot(actb[pl.ds(r0, count), :], w[:, cols], preferred_element_type=F32)
            ebuf[pl.ds(r0, count), cols] = block
            top = jnp.maximum(block[:, :LANES], block[:, LANES:])
            mx[pl.ds(0, count), :] = jnp.maximum(mx[pl.ds(0, count), :], top)
            return carry

        lax.fori_loop(0, vlocal // 256, logits_step, 0)

        def exp_step(b, carry, r0=r0):
            local = pl.ds(pl.multiple_of(b * 32, 32), 32)
            at = pl.ds(pl.multiple_of(r0 + b * 32, 32), 32)
            peak = jnp.max(mx[local, :], axis=1, keepdims=True)
            wide = jnp.broadcast_to(peak, (32, LANES))
            total = jnp.zeros((32, LANES), F32)
            for t in range(vlocal // LANES):
                cols = pl.ds(t * LANES, LANES)
                e = jnp.exp(ebuf[at, cols] - wide)
                ebuf[at, cols] = e
                total = total + e
            total = jnp.sum(total, axis=1, keepdims=True)
            group = b // 4
            lanes = iota((32, LANES), 1)
            stat[at, :] = jnp.where(lanes == group, peak, jnp.where(lanes == group + 4, total, 0.0))
            return carry

        lax.fori_loop(0, count // 32, exp_step, 0)
        packed = stat[pl.ds(r0, LANES), :]
        for b in range(1, 4):
            packed = packed + stat[pl.ds(r0 + b * LANES, LANES), :]
        ssend[h] = packed.T[0:8, :]
        copies = []
        for i in range(1, nz):
            cp = remote(
                ssend.at[h], srecv.at[h, i - 1], stat_ssem.at[h, i - 1], stat_rsem.at[h, i - 1], zpeer(i)
            )
            cp.start()
            copies.append(cp)
        stat_copies.append(copies)

    h_copies = []
    for h in range(2):
        r0 = h * HALF
        count = min(HALF, rows - r0)
        for cp in stat_copies[h]:
            cp.wait()
        mine = ssend[h]
        peak = mine[0:4]
        for i in range(nz - 1):
            peak = jnp.maximum(peak, srecv[h, i][0:4])
        total = mine[4:8] * jnp.exp(mine[0:4] - peak)
        for i in range(nz - 1):
            got = srecv[h, i]
            total = total + got[4:8] * jnp.exp(got[0:4] - peak)
        scol[0:4, :] = jnp.exp(mine[0:4] - peak) / total
        turned = scol[...].T
        for b in range(4):
            at = pl.ds(r0 + b * LANES, LANES)
            frep[at, :] = jnp.broadcast_to(turned[:, b : b + 1], (LANES, LANES)) * coef[at, :]

        def grad_step(b, carry, r0=r0):
            at = pl.ds(pl.multiple_of(r0 + b * 32, 32), 32)
            scale = frep[at, :]
            label = labrep[at, :]
            lcoef = lrep[at, :]
            lanes = iota((32, LANES), 1)
            for t in range(vlocal // LANES):
                cols = pl.ds(t * LANES, LANES)
                value = ebuf[at, cols] * scale - jnp.where(label - t * LANES == lanes, lcoef, 0.0)
                if t == 0:
                    value = value - bl0[at, :]
                gbuf[at, cols] = value.astype(BF16)
            return carry

        lax.fori_loop(0, count // 32, grad_step, 0)

        def hidden_step(n, carry, r0=r0, h=h):
            at = pl.ds(pl.multiple_of(r0 + n * 256, 256), 256)
            part = lax.dot_general(
                w[...], gbuf[at, :], (((1,), (1,)), ((), ())), preferred_element_type=F32
            )
            hsend[h, :, :, pl.ds(pl.multiple_of(n * 256, 256), 256)] = part.astype(BF16).reshape(
                nz, width // nz, 256
            )
            return carry

        lax.fori_loop(0, HALF // 256, hidden_step, 0)
        copies = []
        for i in sorted(range(1, nz), key=lambda i: -min(i, nz - i)):
            cp = remote(
                hsend.at[h, lax.rem(z + i, nz)],
                hrecv.at[h, i - 1],
                h_ssem.at[h, i - 1],
                h_rsem.at[h, i - 1],
                zpeer(i),
            )
            cp.start()
            copies.append(cp)
        h_copies.append(copies)

    chunks = vlocal // WCOLS
    left = pl.ds(0, WCOLS // 2)
    right = pl.ds(WCOLS // 2, WCOLS // 2)
    half_rows = width // 2
    c_copies, p1_copies, p2_copies = [], [], []
    for step in range(chunks + 3):
        if step < chunks:
            c = step
            slot = c % 2
            pbuf[slot] = jnp.dot(
                actp[...], gbuf[:, pl.ds(c * WCOLS, WCOLS)], preferred_element_type=F32
            )
            theirs = pl.ds(pl.multiple_of((1 - core) * half_rows, half_rows), half_rows)
            csend[c] = pbuf[slot, theirs, :].astype(BF16)
            cp = remote(csend.at[c], crecv.at[c], c_ssem.at[c], c_rsem.at[c], partner)
            cp.start()
            c_copies.append(cp)
        if 1 <= step < chunks + 1:
            c = step - 1
            slot = c % 2
            c_copies[c].wait()
            mine = pl.ds(pl.multiple_of(core * half_rows, half_rows), half_rows)
            both = pbuf[slot, mine, :] + crecv[c].astype(F32)
            wsum[c] = both.astype(BF16).reshape(nx, ny, share, WCOLS)
            copies = []
            for i in range(1, nx):
                cp = remote(
                    wsum.at[c, lax.rem(cx + i, nx), :, :, left],
                    xr1.at[c, i - 1],
                    p1_ssem.at[c, i - 1],
                    p1_rsem.at[c, i - 1],
                    xpeer(i),
                )
                cp.start()
                copies.append(cp)
            for i in range(1, ny):
                cp = remote(
                    wsum.at[c, :, lax.rem(cy + i, ny), :, right],
                    yr1.at[c, i - 1],
                    p1_ssem.at[c, wx + i - 1],
                    p1_rsem.at[c, wx + i - 1],
                    ypeer(i),
                )
                cp.start()
                copies.append(cp)
            p1_copies.append(copies)
        if 2 <= step < chunks + 2:
            c = step - 2
            for cp in p1_copies[c]:
                cp.wait()
            total = wsum[c, cx, :, :, left].astype(F32)
            for i in range(wx):
                total = total + xr1[c, i].astype(F32)
            yst32[c] = total
            yst[c] = total.astype(BF16)
            total = wsum[c, :, cy, :, right].astype(F32)
            for i in range(wy):
                total = total + yr1[c, i].astype(F32)
            xst32[c] = total
            xst[c] = total.astype(BF16)
            copies = []
            for i in range(1, ny):
                cp = remote(
                    yst.at[c, lax.rem(cy + i, ny)],
                    yr2.at[c, i - 1],
                    p2_ssem.at[c, i - 1],
                    p2_rsem.at[c, i - 1],
                    ypeer(i),
                )
                cp.start()
                copies.append(cp)
            for i in range(1, nx):
                cp = remote(
                    xst.at[c, lax.rem(cx + i, nx)],
                    xr2.at[c, i - 1],
                    p2_ssem.at[c, wy + i - 1],
                    p2_rsem.at[c, wy + i - 1],
                    xpeer(i),
                )
                cp.start()
                copies.append(cp)
            p2_copies.append(copies)
        if step >= 3:
            c = step - 3
            for cp in p2_copies[c]:
                cp.wait()
            total = yst32[c, cy]
            for i in range(wy):
                total = total + yr2[c, i].astype(F32)
            gw_ref[:, pl.ds(c * WCOLS, WCOLS // 2)] = total
            total = xst32[c, cx]
            for i in range(wx):
                total = total + xr2[c, i].astype(F32)
            gw_ref[:, pl.ds(c * WCOLS + WCOLS // 2, WCOLS // 2)] = total

    slice_rows = width // nz
    act_at = pl.ds(pl.multiple_of(z * slice_rows, slice_rows), slice_rows)
    for h in range(2):
        cols = pl.ds(h * HALF, HALF)
        for cp in h_copies[h]:
            cp.wait()
        total = hsend[h, z].astype(F32)
        for i in range(nz - 1):
            total = total + hrecv[h, i].astype(F32)
        act = actt[act_at, cols]
        agrad[:, cols] = total * (1.0 - act * act)
    grads = agrad[...]
    summed = grads[:, 0:frames]
    for k in range(1, KEPT):
        summed = summed + grads[:, k * frames : (k + 1) * frames]
    ge_ref[...] = summed
    high = grads.astype(BF16)
    low = (grads - high.astype(F32)).astype(BF16)
    slots = jnp.dot(high, picker[...], preferred_element_type=F32) + jnp.dot(
        low, picker[...], preferred_element_type=F32
    )
    gpsend[...] = slots[:, 0:own_rows]
    gp_copy = remote(gpsend, gprecv, gp_sem.at[0], gp_sem.at[1], before)
    gp_copy.start()
    gp_copy.wait()
    gp_ref[...] = (slots[:, own_rows:] + gprecv[...]).T


def body(grid, enc, pred, w, futt, pstart, labels, ulen, bocc, locc, fw):
    nx, ny, nz = grid
    frames, width = enc.shape
    vlocal = w.shape[1]
    slots, depth, _ = pred.shape
    own_rows = slots * depth
    rows_pad = 2 * HALF
    share = width // (nx * ny * 2)
    utts = ulen.shape[0]
    chunks = vlocal // WCOLS
    hw = WCOLS // 2
    vm = pltpu.VMEM
    dma = pltpu.SemaphoreType.DMA
    i32 = jnp.int32
    scratch = [
        vm((frames, width), BF16),
        vm((2 * own_rows, width), BF16),
        vm((width, vlocal), BF16),
        vm((1, frames), i32),
        vm((1, frames), i32),
        vm((KEPT, frames), i32),
        vm((1, utts), i32),
        vm((KEPT, frames), F32),
        vm((KEPT, frames), F32),
        vm((1, frames), F32),
        vm((LANES, 2 * LANES), F32),
        vm((2 * LANES, LANES), F32),
        vm((rows_pad, LANES), i32),
        vm((rows_pad, LANES), F32),
        vm((rows_pad, LANES), F32),
        vm((rows_pad, LANES), F32),
        vm((rows_pad, LANES), F32),
        vm((rows_pad, 2 * own_rows), BF16),
        vm((rows_pad, width), F32),
        vm((rows_pad, width), BF16),
        vm((width, rows_pad), F32),
        vm((width, rows_pad), BF16),
        vm((frames * KEPT, vlocal), F32),
        vm((HALF, LANES), F32),
        vm((rows_pad, LANES), F32),
        vm((2, 8, LANES), F32),
        vm((2, nz - 1, 8, LANES), F32),
        vm((LANES, LANES), F32),
        vm((rows_pad, vlocal), BF16),
        vm((2, nz, width // nz, HALF), BF16),
        vm((2, nz - 1, width // nz, HALF), BF16),
        vm((width // nz, rows_pad), F32),
        vm((2, width, WCOLS), F32),
        vm((chunks, width // 2, WCOLS), BF16),
        vm((chunks, width // 2, WCOLS), BF16),
        vm((chunks, nx, ny, share, WCOLS), BF16),
        vm((chunks, nx - 1, ny, share, hw), BF16),
        vm((chunks, ny, share, hw), BF16),
        vm((chunks, ny, share, hw), F32),
        vm((chunks, ny - 1, share, hw), BF16),
        vm((chunks, ny - 1, nx, share, hw), BF16),
        vm((chunks, nx, share, hw), BF16),
        vm((chunks, nx, share, hw), F32),
        vm((chunks, nx - 1, share, hw), BF16),
        vm((width // nz, own_rows), F32),
        vm((width // nz, own_rows), F32),
        dma((10,)),
        dma((2,)),
        dma((2, nz - 1)),
        dma((2, nz - 1)),
        dma((2, nz - 1)),
        dma((2, nz - 1)),
        dma((chunks,)),
        dma((chunks,)),
        dma((chunks, nx + ny - 2)),
        dma((chunks, nx + ny - 2)),
        dma((chunks, nx + ny - 2)),
        dma((chunks, nx + ny - 2)),
        dma((2,)),
    ]
    gw, ge, gp = pl.pallas_call(
        functools.partial(kernel, grid),
        out_shape=(
            jax.ShapeDtypeStruct((share, vlocal), F32),
            jax.ShapeDtypeStruct((width // nz, frames), F32),
            jax.ShapeDtypeStruct((own_rows, width // nz), F32),
        ),
        in_specs=[pl.BlockSpec(memory_space=pl.ANY)] * 10,
        out_specs=[pl.BlockSpec(memory_space=pltpu.VMEM)] * 3,
        scratch_shapes=scratch,
        compiler_params=pltpu.CompilerParams(
            collective_id=0, has_side_effects=True, vmem_limit_bytes=60 * 2**20
        ),
    )(
        enc,
        pred.reshape(own_rows, width),
        w,
        futt.reshape(1, frames),
        pstart.reshape(1, frames),
        labels.T,
        ulen.reshape(1, utts),
        bocc.T,
        locc.T,
        fw.reshape(1, frames),
    )
    return gw, ge.T, gp.reshape(slots, depth, width // nz)


def solution(mesh, sizes=(4, 4)):
    grid = (sizes[0], sizes[1], mesh.shape["vocab"])
    in_specs = (
        P("dp", None),
        P("dp", None, None),
        P(None, "vocab"),
        P("dp"),
        P("dp"),
        P("dp", None),
        P(),
        P("dp", None),
        P("dp", None),
        P("dp"),
    )
    out_specs = (P("dp", "vocab"), P("dp", "vocab"), P("dp", None, "vocab"))
    return jax.shard_map(
        functools.partial(body, grid), mesh=mesh, in_specs=in_specs, out_specs=out_specs, check_vma=False
    )
```

```python
import functools

import jax
import jax.numpy as jnp
from jax import lax
from jax.experimental import pallas as pl
from jax.experimental.pallas import tpu as pltpu
from jax.sharding import PartitionSpec as P

MESH = pl.DeviceIdType.MESH
F32 = jnp.float32
BF16 = jnp.bfloat16
KEPT = 5
HALF = 512
WCOLS = 768
LCOLS = 1280
EROWS = 64
LANES = 128


def iota(shape, dim):
    return lax.broadcasted_iota(jnp.int32, shape, dim)


def kernel(
    grid,
    enc_hbm,
    pred_hbm,
    w_hbm,
    futt_hbm,
    pstart_hbm,
    labels_hbm,
    ulen_hbm,
    bocc_hbm,
    locc_hbm,
    fw_hbm,
    gw_ref,
    ge_ref,
    gp_ref,
    enc,
    table,
    w,
    futt,
    pstart,
    labels,
    ulen,
    bocc,
    locc,
    fw,
    aux,
    auxt,
    labrep,
    lrep,
    bl0,
    coef,
    frep,
    picker,
    act32,
    actb,
    actt,
    actp,
    ebuf,
    mx,
    sums,
    stat,
    ssend,
    srecv,
    scol,
    gbuf,
    hsend,
    hrecv,
    agrad,
    pbuf,
    csend,
    crecv,
    wsum,
    xr1,
    yst,
    yst32,
    yr2,
    yr1,
    xst,
    xst32,
    xr2,
    gpsend,
    gprecv,
    local_sem,
    pred_sem,
    stat_ssem,
    stat_rsem,
    h_ssem,
    h_rsem,
    c_ssem,
    c_rsem,
    p1_ssem,
    p1_rsem,
    p2_ssem,
    p2_rsem,
    gp_sem,
):
    nx, ny, nz = grid
    ndp = nx * ny * 2
    frames = enc.shape[0]
    rows = frames * KEPT
    width, vlocal = w.shape
    own_rows = pred_hbm.shape[0]
    dp = lax.axis_index("dp")
    z = lax.axis_index("vocab")
    cx = dp // (2 * ny)
    cy = lax.rem(dp // 2, ny)
    core = lax.rem(dp, 2)
    wx = nx - 1
    wy = ny - 1

    def zpeer(i):
        return (dp, lax.rem(z + i, nz))

    def xpeer(i):
        return ((lax.rem(cx + i, nx) * ny + cy) * 2 + core, z)

    def ypeer(i):
        return ((cx * ny + lax.rem(cy + i, ny)) * 2 + core, z)

    partner = (dp + 1 - 2 * core, z)
    following = (lax.rem(dp + 1, ndp), z)
    before = (lax.rem(dp + ndp - 1, ndp), z)

    loads = []
    for i, (src, dst) in enumerate(
        (
            (futt_hbm, futt),
            (pstart_hbm, pstart),
            (labels_hbm, labels),
            (ulen_hbm, ulen),
            (bocc_hbm, bocc),
            (locc_hbm, locc),
            (fw_hbm, fw),
            (enc_hbm, enc),
            (pred_hbm, table.at[pl.ds(own_rows, own_rows)]),
            (w_hbm, w),
        )
    ):
        cp = pltpu.make_async_copy(src, dst, local_sem.at[i])
        cp.start()
        loads.append(cp)

    barrier = pltpu.get_barrier_semaphore()
    peers = [zpeer(i) for i in range(1, nz)] + [xpeer(i) for i in range(1, nx)]
    peers += [ypeer(i) for i in range(1, ny)] + [partner, following, before]
    for peer in peers:
        pl.semaphore_signal(barrier, inc=1, device_id=peer, device_id_type=MESH)

    def remote(src, dst, ssem, rsem, peer):
        return pltpu.make_async_remote_copy(
            src_ref=src, dst_ref=dst, send_sem=ssem, recv_sem=rsem, device_id=peer, device_id_type=MESH
        )

    aux[...] = jnp.zeros_like(aux)
    tail = act32.shape[0] - rows
    act32[pl.ds(rows, tail), :] = jnp.zeros((tail, width), F32)
    gbuf[pl.ds(rows, tail), :] = jnp.zeros((tail, vlocal), BF16)
    picker[pl.ds(rows, tail), :] = jnp.zeros((tail, 2 * own_rows), BF16)
    stat[...] = jnp.zeros_like(stat)
    scol[...] = jnp.zeros_like(scol)
    pl.semaphore_wait(barrier, len(peers))
    pred_copy = remote(
        pred_hbm, table.at[pl.ds(0, own_rows)], pred_sem.at[0], pred_sem.at[1], following
    )
    pred_copy.start()

    for cp in loads[:8]:
        cp.wait()
    aux[0:1, 0:frames] = ((futt[...] - (dp - 1) * (own_rows // 64)) * 64 + pstart[...]).astype(F32)
    aux[1:2, 0:frames] = futt[...].astype(F32)
    aux[2:3, 0:frames] = pstart[...].astype(F32)
    aux[8 : 8 + KEPT, 0:frames] = labels[...].astype(F32)
    aux[16 : 16 + KEPT, 0:frames] = fw[...] * bocc[...]
    aux[24 : 24 + KEPT, 0:frames] = fw[...] * locc[...]
    auxt[...] = aux[...].T

    def column(i):
        return auxt[0:frames, i : i + 1]

    utts = ulen.shape[1]
    futt_col = column(1).astype(jnp.int32)
    found = futt_col == iota((frames, utts), 1)
    limit = jnp.sum(jnp.where(found, ulen[...].astype(F32), 0.0), axis=1, keepdims=True)
    start_col = column(2)
    base_col = column(0).astype(jnp.int32)
    lane = iota((frames, LANES), 1)
    first = jnp.logical_and(lane == 0, z == 0)
    table_iota = iota((frames, 2 * own_rows), 1)
    for k in range(KEPT):
        at = pl.ds(k * frames, frames)
        valid = (start_col + float(k) < limit).astype(F32)
        label_coef = column(24 + k) * valid
        blank_coef = column(16 + k)
        labrep[at, :] = jnp.broadcast_to(column(8 + k).astype(jnp.int32) - z * vlocal, (frames, LANES))
        lrep[at, :] = jnp.broadcast_to(label_coef, (frames, LANES))
        bl0[at, :] = jnp.where(first, jnp.broadcast_to(blank_coef, (frames, LANES)), 0.0)
        coef[at, :] = jnp.broadcast_to(blank_coef + label_coef, (frames, LANES))
        picker[at, :] = (base_col + k == table_iota).astype(BF16)

    loads[8].wait()
    pred_copy.wait()
    for k in range(KEPT):
        at = pl.ds(k * frames, frames)
        picked = jnp.dot(picker[at, :], table[...], preferred_element_type=F32)
        act = jnp.tanh(enc[...].astype(F32) + picked)
        act32[at, :] = act
        actb[at, :] = act.astype(BF16)
    share = width // ndp
    for i in range(act32.shape[0] // LANES):
        cols = pl.ds(i * LANES, LANES)
        turned = act32[cols, :].T
        actt[:, cols] = turned
        split = turned.reshape(nx * ny, 2, share, LANES)
        for c in range(2):
            actp[pl.ds(c * (width // 2), width // 2), cols] = (
                split[:, c].reshape(width // 2, LANES).astype(BF16)
            )

    loads[9].wait()

    stat_copies = []
    for h in range(2):
        r0 = h * HALF
        count = min(HALF, rows - r0)
        mx[...] = jnp.full(mx.shape, -jnp.inf, F32)

        def logits_step(c, carry, r0=r0, count=count):
            cols = pl.ds(pl.multiple_of(c * LCOLS, LCOLS), LCOLS)
            block = jnp.dot(actb[pl.ds(r0, count), :], w[:, cols], preferred_element_type=F32)
            ebuf[pl.ds(r0, count), cols] = block
            top = mx[pl.ds(0, count), :]
            for t in range(LCOLS // LANES):
                top = jnp.maximum(top, block[:, t * LANES : (t + 1) * LANES])
            mx[pl.ds(0, count), :] = top
            return carry

        lax.fori_loop(0, vlocal // LCOLS, logits_step, 0)
        peaks = jnp.max(mx[pl.ds(0, count), :], axis=1, keepdims=True)
        mx[pl.ds(0, count), :] = jnp.broadcast_to(peaks, (count, LANES))

        def exp_step(b, carry, r0=r0):
            local = pl.ds(pl.multiple_of(b * EROWS, EROWS), EROWS)
            at = pl.ds(pl.multiple_of(r0 + b * EROWS, EROWS), EROWS)
            wide = mx[local, :]
            total = jnp.zeros((EROWS, LANES), F32)
            for t in range(vlocal // LANES):
                cols = pl.ds(t * LANES, LANES)
                e = jnp.exp(ebuf[at, cols] - wide)
                ebuf[at, cols] = e
                total = total + e
            sums[local, :] = total
            return carry

        lax.fori_loop(0, count // EROWS, exp_step, 0)
        totals = jnp.sum(sums[pl.ds(0, count), :], axis=1, keepdims=True)
        group = iota((count, LANES), 0) // LANES
        lanes = iota((count, LANES), 1)
        stat[pl.ds(r0, count), :] = jnp.where(
            lanes == group, mx[pl.ds(0, count), :], jnp.where(lanes == group + 4, totals, 0.0)
        )
        packed = stat[pl.ds(r0, LANES), :]
        for b in range(1, 4):
            packed = packed + stat[pl.ds(r0 + b * LANES, LANES), :]
        ssend[h] = packed.T[0:8, :]
        copies = []
        for i in range(1, nz):
            cp = remote(
                ssend.at[h], srecv.at[h, i - 1], stat_ssem.at[h, i - 1], stat_rsem.at[h, i - 1], zpeer(i)
            )
            cp.start()
            copies.append(cp)
        stat_copies.append(copies)

    h_copies = []
    for h in range(2):
        r0 = h * HALF
        count = min(HALF, rows - r0)
        for cp in stat_copies[h]:
            cp.wait()
        mine = ssend[h]
        peak = mine[0:4]
        for i in range(nz - 1):
            peak = jnp.maximum(peak, srecv[h, i][0:4])
        total = mine[4:8] * jnp.exp(mine[0:4] - peak)
        for i in range(nz - 1):
            got = srecv[h, i]
            total = total + got[4:8] * jnp.exp(got[0:4] - peak)
        scol[0:4, :] = jnp.exp(mine[0:4] - peak) / total
        turned = scol[...].T
        for b in range(4):
            at = pl.ds(r0 + b * LANES, LANES)
            frep[at, :] = jnp.broadcast_to(turned[:, b : b + 1], (LANES, LANES)) * coef[at, :]

        def grad_step(b, carry, r0=r0):
            at = pl.ds(pl.multiple_of(r0 + b * 32, 32), 32)
            scale = frep[at, :]
            label = labrep[at, :]
            lcoef = lrep[at, :]
            lanes = iota((32, LANES), 1)
            for t in range(vlocal // LANES):
                cols = pl.ds(t * LANES, LANES)
                value = ebuf[at, cols] * scale - jnp.where(label - t * LANES == lanes, lcoef, 0.0)
                if t == 0:
                    value = value - bl0[at, :]
                gbuf[at, cols] = value.astype(BF16)
            return carry

        lax.fori_loop(0, count // 32, grad_step, 0)

        part = lax.dot_general(
            w[...], gbuf[pl.ds(r0, HALF), :], (((1,), (1,)), ((), ())), preferred_element_type=F32
        )
        hsend[h] = part.astype(BF16).reshape(nz, width // nz, HALF)
        copies = []
        for i in sorted(range(1, nz), key=lambda i: -min(i, nz - i)):
            cp = remote(
                hsend.at[h, lax.rem(z + i, nz)],
                hrecv.at[h, i - 1],
                h_ssem.at[h, i - 1],
                h_rsem.at[h, i - 1],
                zpeer(i),
            )
            cp.start()
            copies.append(cp)
        h_copies.append(copies)

    chunks = vlocal // WCOLS
    left = pl.ds(0, WCOLS // 2)
    right = pl.ds(WCOLS // 2, WCOLS // 2)
    half_rows = width // 2
    c_copies, p1_copies, p2_copies = [], [], []
    for step in range(chunks + 3):
        if step < chunks:
            c = step
            slot = c % 2
            pbuf[slot] = jnp.dot(
                actp[...], gbuf[:, pl.ds(c * WCOLS, WCOLS)], preferred_element_type=F32
            )
            theirs = pl.ds(pl.multiple_of((1 - core) * half_rows, half_rows), half_rows)
            csend[c] = pbuf[slot, theirs, :].astype(BF16)
            cp = remote(csend.at[c], crecv.at[c], c_ssem.at[c], c_rsem.at[c], partner)
            cp.start()
            c_copies.append(cp)
        if 1 <= step < chunks + 1:
            c = step - 1
            slot = c % 2
            c_copies[c].wait()
            mine = pl.ds(pl.multiple_of(core * half_rows, half_rows), half_rows)
            both = pbuf[slot, mine, :] + crecv[c].astype(F32)
            wsum[c] = both.astype(BF16).reshape(nx, ny, share, WCOLS)
            copies = []
            for i in range(1, nx):
                cp = remote(
                    wsum.at[c, lax.rem(cx + i, nx), :, :, left],
                    xr1.at[c, i - 1],
                    p1_ssem.at[c, i - 1],
                    p1_rsem.at[c, i - 1],
                    xpeer(i),
                )
                cp.start()
                copies.append(cp)
            for i in range(1, ny):
                cp = remote(
                    wsum.at[c, :, lax.rem(cy + i, ny), :, right],
                    yr1.at[c, i - 1],
                    p1_ssem.at[c, wx + i - 1],
                    p1_rsem.at[c, wx + i - 1],
                    ypeer(i),
                )
                cp.start()
                copies.append(cp)
            p1_copies.append(copies)
        if step == chunks:
            slice_rows = width // nz
            act_at = pl.ds(pl.multiple_of(z * slice_rows, slice_rows), slice_rows)
            for h in range(2):
                cols = pl.ds(h * HALF, HALF)
                for cp in h_copies[h]:
                    cp.wait()
                total = hsend[h, z].astype(F32)
                for i in range(nz - 1):
                    total = total + hrecv[h, i].astype(F32)
                act = actt[act_at, cols]
                agrad[:, cols] = total * (1.0 - act * act)
            grads = agrad[...]
            summed = grads[:, 0:frames]
            for k in range(1, KEPT):
                summed = summed + grads[:, k * frames : (k + 1) * frames]
            ge_ref[...] = summed
            high = grads.astype(BF16)
            low = (grads - high.astype(F32)).astype(BF16)
            slots = jnp.dot(high, picker[...], preferred_element_type=F32) + jnp.dot(
                low, picker[...], preferred_element_type=F32
            )
            gpsend[...] = slots[:, 0:own_rows]
            gp_copy = remote(gpsend, gprecv, gp_sem.at[0], gp_sem.at[1], before)
            gp_copy.start()
        if 2 <= step < chunks + 2:
            c = step - 2
            for cp in p1_copies[c]:
                cp.wait()
            total = wsum[c, cx, :, :, left].astype(F32)
            for i in range(wx):
                total = total + xr1[c, i].astype(F32)
            yst32[c] = total
            yst[c] = total.astype(BF16)
            total = wsum[c, :, cy, :, right].astype(F32)
            for i in range(wy):
                total = total + yr1[c, i].astype(F32)
            xst32[c] = total
            xst[c] = total.astype(BF16)
            copies = []
            for i in range(1, ny):
                cp = remote(
                    yst.at[c, lax.rem(cy + i, ny)],
                    yr2.at[c, i - 1],
                    p2_ssem.at[c, i - 1],
                    p2_rsem.at[c, i - 1],
                    ypeer(i),
                )
                cp.start()
                copies.append(cp)
            for i in range(1, nx):
                cp = remote(
                    xst.at[c, lax.rem(cx + i, nx)],
                    xr2.at[c, i - 1],
                    p2_ssem.at[c, wy + i - 1],
                    p2_rsem.at[c, wy + i - 1],
                    xpeer(i),
                )
                cp.start()
                copies.append(cp)
            p2_copies.append(copies)
        if step >= 3:
            c = step - 3
            for cp in p2_copies[c]:
                cp.wait()
            total = yst32[c, cy]
            for i in range(wy):
                total = total + yr2[c, i].astype(F32)
            gw_ref[:, pl.ds(c * WCOLS, WCOLS // 2)] = total
            total = xst32[c, cx]
            for i in range(wx):
                total = total + xr2[c, i].astype(F32)
            gw_ref[:, pl.ds(c * WCOLS + WCOLS // 2, WCOLS // 2)] = total

    gp_copy.wait()
    gp_ref[...] = (slots[:, own_rows:] + gprecv[...]).T


def handover(*refs):
    sems = refs[6]
    copies = [pltpu.make_async_copy(refs[i], refs[3 + i], sems.at[i]) for i in range(3)]
    for cp in copies:
        cp.start()
    for cp in copies:
        cp.wait()


def body(grid, enc, pred, w, futt, pstart, labels, ulen, bocc, locc, fw):
    nx, ny, nz = grid
    frames, width = enc.shape
    vlocal = w.shape[1]
    slots, depth, _ = pred.shape
    own_rows = slots * depth
    rows_pad = 2 * HALF
    share = width // (nx * ny * 2)
    utts = ulen.shape[0]
    chunks = vlocal // WCOLS
    hw = WCOLS // 2
    vm = pltpu.VMEM
    dma = pltpu.SemaphoreType.DMA
    i32 = jnp.int32
    scratch = [
        vm((frames, width), BF16),
        vm((2 * own_rows, width), BF16),
        vm((width, vlocal), BF16),
        vm((1, frames), i32),
        vm((1, frames), i32),
        vm((KEPT, frames), i32),
        vm((1, utts), i32),
        vm((KEPT, frames), F32),
        vm((KEPT, frames), F32),
        vm((1, frames), F32),
        vm((LANES, 2 * LANES), F32),
        vm((2 * LANES, LANES), F32),
        vm((rows_pad, LANES), i32),
        vm((rows_pad, LANES), F32),
        vm((rows_pad, LANES), F32),
        vm((rows_pad, LANES), F32),
        vm((rows_pad, LANES), F32),
        vm((rows_pad, 2 * own_rows), BF16),
        vm((rows_pad, width), F32),
        vm((rows_pad, width), BF16),
        vm((width, rows_pad), F32),
        vm((width, rows_pad), BF16),
        vm((frames * KEPT, vlocal), F32),
        vm((HALF, LANES), F32),
        vm((HALF, LANES), F32),
        vm((rows_pad, LANES), F32),
        vm((2, 8, LANES), F32),
        vm((2, nz - 1, 8, LANES), F32),
        vm((LANES, LANES), F32),
        vm((rows_pad, vlocal), BF16),
        vm((2, nz, width // nz, HALF), BF16),
        vm((2, nz - 1, width // nz, HALF), BF16),
        vm((width // nz, rows_pad), F32),
        vm((2, width, WCOLS), F32),
        vm((chunks, width // 2, WCOLS), BF16),
        vm((chunks, width // 2, WCOLS), BF16),
        vm((chunks, nx, ny, share, WCOLS), BF16),
        vm((chunks, nx - 1, ny, share, hw), BF16),
        vm((chunks, ny, share, hw), BF16),
        vm((chunks, ny, share, hw), F32),
        vm((chunks, ny - 1, share, hw), BF16),
        vm((chunks, ny - 1, nx, share, hw), BF16),
        vm((chunks, nx, share, hw), BF16),
        vm((chunks, nx, share, hw), F32),
        vm((chunks, nx - 1, share, hw), BF16),
        vm((width // nz, own_rows), F32),
        vm((width // nz, own_rows), F32),
        dma((10,)),
        dma((2,)),
        dma((2, nz - 1)),
        dma((2, nz - 1)),
        dma((2, nz - 1)),
        dma((2, nz - 1)),
        dma((chunks,)),
        dma((chunks,)),
        dma((chunks, nx + ny - 2)),
        dma((chunks, nx + ny - 2)),
        dma((chunks, nx + ny - 2)),
        dma((chunks, nx + ny - 2)),
        dma((2,)),
    ]
    results = pl.pallas_call(
        functools.partial(kernel, grid),
        out_shape=(
            jax.ShapeDtypeStruct((share, vlocal), F32),
            jax.ShapeDtypeStruct((width // nz, frames), F32),
            jax.ShapeDtypeStruct((own_rows, width // nz), F32),
        ),
        in_specs=[pl.BlockSpec(memory_space=pl.ANY)] * 10,
        out_specs=[pl.BlockSpec(memory_space=pltpu.VMEM)] * 3,
        scratch_shapes=scratch,
        compiler_params=pltpu.CompilerParams(
            collective_id=0, has_side_effects=True, vmem_limit_bytes=60 * 2**20
        ),
    )(
        enc,
        pred.reshape(own_rows, width),
        w,
        futt.reshape(1, frames),
        pstart.reshape(1, frames),
        labels.T,
        ulen.reshape(1, utts),
        bocc.T,
        locc.T,
        fw.reshape(1, frames),
    )
    gw, ge, gp = pl.pallas_call(
        handover,
        out_shape=tuple(jax.ShapeDtypeStruct(r.shape, r.dtype) for r in results),
        in_specs=[pl.BlockSpec(memory_space=pltpu.VMEM)] * 3,
        out_specs=[pl.BlockSpec(memory_space=pl.ANY)] * 3,
        scratch_shapes=[dma((3,))],
    )(*results)
    return gw, ge.T, gp.reshape(slots, depth, width // nz)


def solution(mesh, sizes=(4, 4)):
    grid = (sizes[0], sizes[1], mesh.shape["vocab"])
    in_specs = (
        P("dp", None),
        P("dp", None, None),
        P(None, "vocab"),
        P("dp"),
        P("dp"),
        P("dp", None),
        P(),
        P("dp", None),
        P("dp", None),
        P("dp"),
    )
    out_specs = (P("dp", "vocab"), P("dp", "vocab"), P("dp", None, "vocab"))
    return jax.shard_map(
        functools.partial(body, grid), mesh=mesh, in_specs=in_specs, out_specs=out_specs, check_vma=False
    )
```

```python
import functools

import jax
import jax.numpy as jnp
from jax import lax
from jax.experimental import pallas as pl
from jax.experimental.pallas import tpu as pltpu
from jax.sharding import PartitionSpec as P

MESH = pl.DeviceIdType.MESH
F32 = jnp.float32
BF16 = jnp.bfloat16
KEPT = 5
HALF = 512
WCOLS = 768
LCOLS = 1280
EROWS = 64
LANES = 128


def iota(shape, dim):
    return lax.broadcasted_iota(jnp.int32, shape, dim)


def kernel(
    grid,
    enc_hbm,
    pred_hbm,
    w_hbm,
    futt_hbm,
    pstart_hbm,
    labels_hbm,
    ulen_hbm,
    bocc_hbm,
    locc_hbm,
    fw_hbm,
    gw_ref,
    ge_ref,
    gp_ref,
    enc,
    table,
    w,
    futt,
    pstart,
    labels,
    ulen,
    bocc,
    locc,
    fw,
    aux,
    auxt,
    labrep,
    lrep,
    bl0,
    coef,
    frep,
    picker,
    act32,
    actb,
    actt,
    actp,
    ebuf,
    mx,
    sums,
    stat,
    ssend,
    srecv,
    scol,
    gbuf,
    hsend,
    far,
    half_far,
    near,
    relayed,
    rsend,
    agrad,
    pbuf,
    csend,
    crecv,
    wsum,
    xr1,
    yst,
    yst32,
    yr2,
    yr1,
    xst,
    xst32,
    xr2,
    gpsend,
    gprecv,
    local_sem,
    pred_sem,
    stat_ssem,
    stat_rsem,
    h_ssem,
    h_rsem,
    c_ssem,
    c_rsem,
    p1_ssem,
    p1_rsem,
    p2_ssem,
    p2_rsem,
    gp_sem,
):
    nx, ny, nz = grid
    ndp = nx * ny * 2
    frames = enc.shape[0]
    rows = frames * KEPT
    width, vlocal = w.shape
    own_rows = pred_hbm.shape[0]
    dp = lax.axis_index("dp")
    z = lax.axis_index("vocab")
    cx = dp // (2 * ny)
    cy = lax.rem(dp // 2, ny)
    core = lax.rem(dp, 2)
    wx = nx - 1
    wy = ny - 1

    def zpeer(i):
        return (dp, lax.rem(z + i, nz))

    def xpeer(i):
        return ((lax.rem(cx + i, nx) * ny + cy) * 2 + core, z)

    def ypeer(i):
        return ((cx * ny + lax.rem(cy + i, ny)) * 2 + core, z)

    partner = (dp + 1 - 2 * core, z)
    following = (lax.rem(dp + 1, ndp), z)
    before = (lax.rem(dp + ndp - 1, ndp), z)

    loads = []
    for i, (src, dst) in enumerate(
        (
            (futt_hbm, futt),
            (pstart_hbm, pstart),
            (labels_hbm, labels),
            (ulen_hbm, ulen),
            (bocc_hbm, bocc),
            (locc_hbm, locc),
            (fw_hbm, fw),
            (enc_hbm, enc),
            (pred_hbm, table.at[pl.ds(own_rows, own_rows)]),
            (w_hbm, w),
        )
    ):
        cp = pltpu.make_async_copy(src, dst, local_sem.at[i])
        cp.start()
        loads.append(cp)

    barrier = pltpu.get_barrier_semaphore()
    peers = [zpeer(i) for i in range(1, nz)] + [xpeer(i) for i in range(1, nx)]
    peers += [ypeer(i) for i in range(1, ny)] + [partner, following, before]
    for peer in peers:
        pl.semaphore_signal(barrier, inc=1, device_id=peer, device_id_type=MESH)

    def remote(src, dst, ssem, rsem, peer):
        return pltpu.make_async_remote_copy(
            src_ref=src, dst_ref=dst, send_sem=ssem, recv_sem=rsem, device_id=peer, device_id_type=MESH
        )

    aux[...] = jnp.zeros_like(aux)
    tail = act32.shape[0] - rows
    act32[pl.ds(rows, tail), :] = jnp.zeros((tail, width), F32)
    gbuf[pl.ds(rows, tail), :] = jnp.zeros((tail, vlocal), BF16)
    picker[pl.ds(rows, tail), :] = jnp.zeros((tail, 2 * own_rows), BF16)
    stat[...] = jnp.zeros_like(stat)
    scol[...] = jnp.zeros_like(scol)
    pl.semaphore_wait(barrier, len(peers))
    pred_copy = remote(
        pred_hbm, table.at[pl.ds(0, own_rows)], pred_sem.at[0], pred_sem.at[1], following
    )
    pred_copy.start()

    for cp in loads[:8]:
        cp.wait()
    aux[0:1, 0:frames] = ((futt[...] - (dp - 1) * (own_rows // 64)) * 64 + pstart[...]).astype(F32)
    aux[1:2, 0:frames] = futt[...].astype(F32)
    aux[2:3, 0:frames] = pstart[...].astype(F32)
    aux[8 : 8 + KEPT, 0:frames] = labels[...].astype(F32)
    aux[16 : 16 + KEPT, 0:frames] = fw[...] * bocc[...]
    aux[24 : 24 + KEPT, 0:frames] = fw[...] * locc[...]
    auxt[...] = aux[...].T

    def column(i):
        return auxt[0:frames, i : i + 1]

    utts = ulen.shape[1]
    futt_col = column(1).astype(jnp.int32)
    found = futt_col == iota((frames, utts), 1)
    limit = jnp.sum(jnp.where(found, ulen[...].astype(F32), 0.0), axis=1, keepdims=True)
    start_col = column(2)
    base_col = column(0).astype(jnp.int32)
    lane = iota((frames, LANES), 1)
    first = jnp.logical_and(lane == 0, z == 0)
    table_iota = iota((frames, 2 * own_rows), 1)
    for k in range(KEPT):
        at = pl.ds(k * frames, frames)
        valid = (start_col + float(k) < limit).astype(F32)
        label_coef = column(24 + k) * valid
        blank_coef = column(16 + k)
        labrep[at, :] = jnp.broadcast_to(column(8 + k).astype(jnp.int32) - z * vlocal, (frames, LANES))
        lrep[at, :] = jnp.broadcast_to(label_coef, (frames, LANES))
        bl0[at, :] = jnp.where(first, jnp.broadcast_to(blank_coef, (frames, LANES)), 0.0)
        coef[at, :] = jnp.broadcast_to(blank_coef + label_coef, (frames, LANES))
        picker[at, :] = (base_col + k == table_iota).astype(BF16)

    loads[8].wait()
    pred_copy.wait()
    for k in range(KEPT):
        at = pl.ds(k * frames, frames)
        picked = jnp.dot(picker[at, :], table[...], preferred_element_type=F32)
        act = jnp.tanh(enc[...].astype(F32) + picked)
        act32[at, :] = act
        actb[at, :] = act.astype(BF16)
    share = width // ndp
    for i in range(act32.shape[0] // LANES):
        cols = pl.ds(i * LANES, LANES)
        turned = act32[cols, :].T
        actt[:, cols] = turned
        split = turned.reshape(nx * ny, 2, share, LANES)
        for c in range(2):
            actp[pl.ds(c * (width // 2), width // 2), cols] = (
                split[:, c].reshape(width // 2, LANES).astype(BF16)
            )

    loads[9].wait()

    stat_copies = []
    for h in range(2):
        r0 = h * HALF
        count = min(HALF, rows - r0)
        mx[...] = jnp.full(mx.shape, -jnp.inf, F32)

        def logits_step(c, carry, r0=r0, count=count):
            cols = pl.ds(pl.multiple_of(c * LCOLS, LCOLS), LCOLS)
            block = jnp.dot(actb[pl.ds(r0, count), :], w[:, cols], preferred_element_type=F32)
            ebuf[pl.ds(r0, count), cols] = block
            top = mx[pl.ds(0, count), :]
            for t in range(LCOLS // LANES):
                top = jnp.maximum(top, block[:, t * LANES : (t + 1) * LANES])
            mx[pl.ds(0, count), :] = top
            return carry

        lax.fori_loop(0, vlocal // LCOLS, logits_step, 0)
        peaks = jnp.max(mx[pl.ds(0, count), :], axis=1, keepdims=True)
        mx[pl.ds(0, count), :] = jnp.broadcast_to(peaks, (count, LANES))

        def exp_step(b, carry, r0=r0):
            local = pl.ds(pl.multiple_of(b * EROWS, EROWS), EROWS)
            at = pl.ds(pl.multiple_of(r0 + b * EROWS, EROWS), EROWS)
            wide = mx[local, :]
            total = jnp.zeros((EROWS, LANES), F32)
            for t in range(vlocal // LANES):
                cols = pl.ds(t * LANES, LANES)
                e = jnp.exp(ebuf[at, cols] - wide)
                ebuf[at, cols] = e
                total = total + e
            sums[local, :] = total
            return carry

        lax.fori_loop(0, count // EROWS, exp_step, 0)
        totals = jnp.sum(sums[pl.ds(0, count), :], axis=1, keepdims=True)
        group = iota((count, LANES), 0) // LANES
        lanes = iota((count, LANES), 1)
        stat[pl.ds(r0, count), :] = jnp.where(
            lanes == group, mx[pl.ds(0, count), :], jnp.where(lanes == group + 4, totals, 0.0)
        )
        packed = stat[pl.ds(r0, LANES), :]
        for b in range(1, 4):
            packed = packed + stat[pl.ds(r0 + b * LANES, LANES), :]
        ssend[h] = packed.T[0:8, :]
        copies = []
        for i in range(1, nz):
            cp = remote(
                ssend.at[h], srecv.at[h, i - 1], stat_ssem.at[h, i - 1], stat_rsem.at[h, i - 1], zpeer(i)
            )
            cp.start()
            copies.append(cp)
        stat_copies.append(copies)

    slice_rows = width // nz

    def grad_half(h):
        r0 = h * HALF
        count = min(HALF, rows - r0)
        for cp in stat_copies[h]:
            cp.wait()
        mine = ssend[h]
        peak = mine[0:4]
        for i in range(nz - 1):
            peak = jnp.maximum(peak, srecv[h, i][0:4])
        total = mine[4:8] * jnp.exp(mine[0:4] - peak)
        for i in range(nz - 1):
            got = srecv[h, i]
            total = total + got[4:8] * jnp.exp(got[0:4] - peak)
        scol[0:4, :] = jnp.exp(mine[0:4] - peak) / total
        turned = scol[...].T
        for b in range(4):
            at = pl.ds(r0 + b * LANES, LANES)
            frep[at, :] = jnp.broadcast_to(turned[:, b : b + 1], (LANES, LANES)) * coef[at, :]

        def grad_step(b, carry):
            at = pl.ds(pl.multiple_of(r0 + b * 32, 32), 32)
            scale = frep[at, :]
            label = labrep[at, :]
            lcoef = lrep[at, :]
            lanes = iota((32, LANES), 1)
            for t in range(vlocal // LANES):
                cols = pl.ds(t * LANES, LANES)
                value = ebuf[at, cols] * scale - jnp.where(label - t * LANES == lanes, lcoef, 0.0)
                if t == 0:
                    value = value - bl0[at, :]
                gbuf[at, cols] = value.astype(BF16)
            return carry

        lax.fori_loop(0, count // 32, grad_step, 0)

    h_copies = {}
    relay_copies = {}

    def hidden_half(h):
        r0 = h * HALF
        part = lax.dot_general(
            w[...], gbuf[pl.ds(r0, HALF), :], (((1,), (1,)), ((), ())), preferred_element_type=F32
        )
        hsend[h] = part.astype(BF16).reshape(nz, slice_rows, HALF)
        copies = []
        quarter = HALF // 2
        plan = [
            (hsend.at[h, lax.rem(z + 4, nz), :, pl.ds(0, quarter)], half_far.at[h, 0], 2),
            (hsend.at[h, lax.rem(z + 4, nz), :, pl.ds(quarter, quarter)], half_far.at[h, 1], nz - 2),
            (hsend.at[h, lax.rem(z + 3, nz)], far.at[h, 0], 1),
            (hsend.at[h, lax.rem(z + nz - 3, nz)], far.at[h, 1], nz - 1),
            (hsend.at[h, lax.rem(z + 1, nz)], near.at[h, 0], 1),
            (hsend.at[h, lax.rem(z + nz - 1, nz)], near.at[h, 1], nz - 1),
        ]
        for n, (src, dst, shift) in enumerate(plan):
            cp = remote(src, dst, h_ssem.at[h, n], h_rsem.at[h, n], zpeer(shift))
            cp.start()
            copies.append(cp)
        h_copies[h] = copies

    def relay_half(h):
        copies = []
        quarter = HALF // 2
        for side, shift in ((0, 2), (1, nz - 2)):
            h_copies[h][side].wait()
            h_copies[h][2 + side].wait()
            own = lax.rem(z + shift, nz)
            for part in range(2):
                cols = pl.ds(part * quarter, quarter)
                total = hsend[h, own, :, cols].astype(F32) + far[h, side, :, cols].astype(F32)
                if part == side:
                    total = total + half_far[h, side].astype(F32)
                rsend[h, side, :, cols] = total.astype(BF16)
            cp = remote(
                rsend.at[h, side],
                relayed.at[h, side],
                h_ssem.at[h, 6 + side],
                h_rsem.at[h, 6 + side],
                zpeer(shift),
            )
            cp.start()
            copies.append(cp)
        relay_copies[h] = copies

    def hidden_finish():
        act_at = pl.ds(pl.multiple_of(z * slice_rows, slice_rows), slice_rows)
        for h in range(2):
            cols = pl.ds(h * HALF, HALF)
            for cp in h_copies[h][4:] + relay_copies[h]:
                cp.wait()
            total = hsend[h, z].astype(F32)
            for i in range(2):
                total = total + near[h, i].astype(F32) + relayed[h, i].astype(F32)
            act = actt[act_at, cols]
            agrad[:, cols] = total * (1.0 - act * act)
        grads = agrad[...]
        summed = grads[:, 0:frames]
        for k in range(1, KEPT):
            summed = summed + grads[:, k * frames : (k + 1) * frames]
        ge_ref[...] = summed
        high = grads.astype(BF16)
        low = (grads - high.astype(F32)).astype(BF16)
        slots = jnp.dot(high, picker[...], preferred_element_type=F32) + jnp.dot(
            low, picker[...], preferred_element_type=F32
        )
        gpsend[...] = slots[:, 0:own_rows]
        gp_copy = remote(gpsend, gprecv, gp_sem.at[0], gp_sem.at[1], before)
        gp_copy.start()
        return slots, gp_copy

    chunks = vlocal // WCOLS
    left = pl.ds(0, WCOLS // 2)
    right = pl.ds(WCOLS // 2, WCOLS // 2)
    half_rows = width // 2
    c_copies, p1_copies, p2_copies = {}, {}, {}

    def weight_chunk(c):
        slot = c % 3
        pbuf[slot] = jnp.dot(
            actp[...], gbuf[:, pl.ds(c * WCOLS, WCOLS)], preferred_element_type=F32
        )
        theirs = pl.ds(pl.multiple_of((1 - core) * half_rows, half_rows), half_rows)
        csend[c] = pbuf[slot, theirs, :].astype(BF16)
        cp = remote(csend.at[c], crecv.at[c], c_ssem.at[c], c_rsem.at[c], partner)
        cp.start()
        c_copies[c] = cp

    def weight_first(c):
        c_copies[c].wait()
        mine = pl.ds(pl.multiple_of(core * half_rows, half_rows), half_rows)
        both = pbuf[c % 3, mine, :] + crecv[c].astype(F32)
        wsum[c] = both.astype(BF16).reshape(nx, ny, share, WCOLS)
        copies = []
        for i in sorted(range(1, nx), key=lambda i: -min(i, nx - i)):
            cp = remote(
                wsum.at[c, lax.rem(cx + i, nx), :, :, left],
                xr1.at[c, i - 1],
                p1_ssem.at[c, i - 1],
                p1_rsem.at[c, i - 1],
                xpeer(i),
            )
            cp.start()
            copies.append(cp)
        for i in sorted(range(1, ny), key=lambda i: -min(i, ny - i)):
            cp = remote(
                wsum.at[c, :, lax.rem(cy + i, ny), :, right],
                yr1.at[c, i - 1],
                p1_ssem.at[c, wx + i - 1],
                p1_rsem.at[c, wx + i - 1],
                ypeer(i),
            )
            cp.start()
            copies.append(cp)
        p1_copies[c] = copies

    def weight_second(c):
        for cp in p1_copies[c]:
            cp.wait()
        total = wsum[c, cx, :, :, left].astype(F32)
        for i in range(wx):
            total = total + xr1[c, i].astype(F32)
        yst32[c] = total
        yst[c] = total.astype(BF16)
        total = wsum[c, :, cy, :, right].astype(F32)
        for i in range(wy):
            total = total + yr1[c, i].astype(F32)
        xst32[c] = total
        xst[c] = total.astype(BF16)
        copies = []
        for i in range(1, ny):
            cp = remote(
                yst.at[c, lax.rem(cy + i, ny)],
                yr2.at[c, i - 1],
                p2_ssem.at[c, i - 1],
                p2_rsem.at[c, i - 1],
                ypeer(i),
            )
            cp.start()
            copies.append(cp)
        for i in range(1, nx):
            cp = remote(
                xst.at[c, lax.rem(cx + i, nx)],
                xr2.at[c, i - 1],
                p2_ssem.at[c, wy + i - 1],
                p2_rsem.at[c, wy + i - 1],
                xpeer(i),
            )
            cp.start()
            copies.append(cp)
        p2_copies[c] = copies

    def weight_last(c):
        for cp in p2_copies[c]:
            cp.wait()
        total = yst32[c, cy]
        for i in range(wy):
            total = total + yr2[c, i].astype(F32)
        gw_ref[:, pl.ds(c * WCOLS, WCOLS // 2)] = total
        total = xst32[c, cx]
        for i in range(wx):
            total = total + xr2[c, i].astype(F32)
        gw_ref[:, pl.ds(c * WCOLS + WCOLS // 2, WCOLS // 2)] = total

    grad_half(0)
    hidden_half(0)
    grad_half(1)
    weight_chunk(0)
    weight_chunk(1)
    weight_first(0)
    hidden_half(1)
    relay_half(0)
    for c in range(2, chunks):
        weight_chunk(c)
        weight_first(c - 1)
    weight_second(0)
    weight_first(chunks - 1)
    relay_half(1)
    for c in range(1, chunks - 1):
        weight_second(c)
    slots, gp_copy = hidden_finish()
    weight_second(chunks - 1)
    for c in range(chunks):
        weight_last(c)
    gp_copy.wait()
    gp_ref[...] = (slots[:, own_rows:] + gprecv[...]).T


def handover(*refs):
    sems = refs[6]
    copies = [pltpu.make_async_copy(refs[i], refs[3 + i], sems.at[i]) for i in range(3)]
    for cp in copies:
        cp.start()
    for cp in copies:
        cp.wait()


def body(grid, enc, pred, w, futt, pstart, labels, ulen, bocc, locc, fw):
    nx, ny, nz = grid
    frames, width = enc.shape
    vlocal = w.shape[1]
    slots, depth, _ = pred.shape
    own_rows = slots * depth
    rows_pad = 2 * HALF
    share = width // (nx * ny * 2)
    utts = ulen.shape[0]
    chunks = vlocal // WCOLS
    hw = WCOLS // 2
    vm = pltpu.VMEM
    dma = pltpu.SemaphoreType.DMA
    i32 = jnp.int32
    scratch = [
        vm((frames, width), BF16),
        vm((2 * own_rows, width), BF16),
        vm((width, vlocal), BF16),
        vm((1, frames), i32),
        vm((1, frames), i32),
        vm((KEPT, frames), i32),
        vm((1, utts), i32),
        vm((KEPT, frames), F32),
        vm((KEPT, frames), F32),
        vm((1, frames), F32),
        vm((LANES, 2 * LANES), F32),
        vm((2 * LANES, LANES), F32),
        vm((rows_pad, LANES), i32),
        vm((rows_pad, LANES), F32),
        vm((rows_pad, LANES), F32),
        vm((rows_pad, LANES), F32),
        vm((rows_pad, LANES), F32),
        vm((rows_pad, 2 * own_rows), BF16),
        vm((rows_pad, width), F32),
        vm((rows_pad, width), BF16),
        vm((width, rows_pad), F32),
        vm((width, rows_pad), BF16),
        vm((frames * KEPT, vlocal), F32),
        vm((HALF, LANES), F32),
        vm((HALF, LANES), F32),
        vm((rows_pad, LANES), F32),
        vm((2, 8, LANES), F32),
        vm((2, nz - 1, 8, LANES), F32),
        vm((LANES, LANES), F32),
        vm((rows_pad, vlocal), BF16),
        vm((2, nz, width // nz, HALF), BF16),
        vm((2, 2, width // nz, HALF), BF16),
        vm((2, 2, width // nz, HALF // 2), BF16),
        vm((2, 2, width // nz, HALF), BF16),
        vm((2, 2, width // nz, HALF), BF16),
        vm((2, 2, width // nz, HALF), BF16),
        vm((width // nz, rows_pad), F32),
        vm((3, width, WCOLS), F32),
        vm((chunks, width // 2, WCOLS), BF16),
        vm((chunks, width // 2, WCOLS), BF16),
        vm((chunks, nx, ny, share, WCOLS), BF16),
        vm((chunks, nx - 1, ny, share, hw), BF16),
        vm((chunks, ny, share, hw), BF16),
        vm((chunks, ny, share, hw), F32),
        vm((chunks, ny - 1, share, hw), BF16),
        vm((chunks, ny - 1, nx, share, hw), BF16),
        vm((chunks, nx, share, hw), BF16),
        vm((chunks, nx, share, hw), F32),
        vm((chunks, nx - 1, share, hw), BF16),
        vm((width // nz, own_rows), F32),
        vm((width // nz, own_rows), F32),
        dma((10,)),
        dma((2,)),
        dma((2, nz - 1)),
        dma((2, nz - 1)),
        dma((2, 8)),
        dma((2, 8)),
        dma((chunks,)),
        dma((chunks,)),
        dma((chunks, nx + ny - 2)),
        dma((chunks, nx + ny - 2)),
        dma((chunks, nx + ny - 2)),
        dma((chunks, nx + ny - 2)),
        dma((2,)),
    ]
    results = pl.pallas_call(
        functools.partial(kernel, grid),
        out_shape=(
            jax.ShapeDtypeStruct((share, vlocal), F32),
            jax.ShapeDtypeStruct((width // nz, frames), F32),
            jax.ShapeDtypeStruct((own_rows, width // nz), F32),
        ),
        in_specs=[pl.BlockSpec(memory_space=pl.ANY)] * 10,
        out_specs=[pl.BlockSpec(memory_space=pltpu.VMEM)] * 3,
        scratch_shapes=scratch,
        compiler_params=pltpu.CompilerParams(
            collective_id=0, has_side_effects=True, vmem_limit_bytes=60 * 2**20
        ),
    )(
        enc,
        pred.reshape(own_rows, width),
        w,
        futt.reshape(1, frames),
        pstart.reshape(1, frames),
        labels.T,
        ulen.reshape(1, utts),
        bocc.T,
        locc.T,
        fw.reshape(1, frames),
    )
    gw, ge, gp = pl.pallas_call(
        handover,
        out_shape=tuple(jax.ShapeDtypeStruct(r.shape, r.dtype) for r in results),
        in_specs=[pl.BlockSpec(memory_space=pltpu.VMEM)] * 3,
        out_specs=[pl.BlockSpec(memory_space=pl.ANY)] * 3,
        scratch_shapes=[dma((3,))],
    )(*results)
    return gw, ge.T, gp.reshape(slots, depth, width // nz)


def solution(mesh, sizes=(4, 4)):
    grid = (sizes[0], sizes[1], mesh.shape["vocab"])
    in_specs = (
        P("dp", None),
        P("dp", None, None),
        P(None, "vocab"),
        P("dp"),
        P("dp"),
        P("dp", None),
        P(),
        P("dp", None),
        P("dp", None),
        P("dp"),
    )
    out_specs = (P("dp", "vocab"), P("dp", "vocab"), P("dp", None, "vocab"))
    return jax.shard_map(
        functools.partial(body, grid), mesh=mesh, in_specs=in_specs, out_specs=out_specs, check_vma=False
    )
```

```python
import functools

import jax
import jax.numpy as jnp
from jax import lax
from jax.experimental import pallas as pl
from jax.experimental.pallas import tpu as pltpu
from jax.sharding import PartitionSpec as P

MESH = pl.DeviceIdType.MESH
F32 = jnp.float32
BF16 = jnp.bfloat16
KEPT = 5
HALF = 512
WCOLS = 768
LCOLS = 1280
EROWS = 64
LANES = 128


def iota(shape, dim):
    return lax.broadcasted_iota(jnp.int32, shape, dim)


def kernel(
    grid,
    enc_hbm,
    pred_hbm,
    w_hbm,
    futt_hbm,
    pstart_hbm,
    labels_hbm,
    ulen_hbm,
    bocc_hbm,
    locc_hbm,
    fw_hbm,
    gw_ref,
    ge_ref,
    gp_ref,
    enc,
    table,
    w,
    futt,
    pstart,
    labels,
    ulen,
    bocc,
    locc,
    fw,
    aux,
    auxt,
    labrep,
    lrep,
    bl0,
    coef,
    frep,
    picker,
    act32,
    actb,
    actt,
    actp,
    ebuf,
    mx,
    sums,
    stat,
    ssend,
    srecv,
    scol,
    gbuf,
    hsum,
    hsend,
    far,
    half_far,
    near,
    relayed,
    rsend,
    agrad,
    pbuf,
    csend,
    crecv,
    wleft,
    wright,
    xr1,
    yst,
    yst32,
    yr2,
    yr1,
    xst,
    xst32,
    xr2,
    gpsend,
    gprecv,
    local_sem,
    pred_sem,
    stat_ssem,
    stat_rsem,
    h_ssem,
    h_rsem,
    c_ssem,
    c_rsem,
    p1_ssem,
    p1_rsem,
    p2_ssem,
    p2_rsem,
    gp_sem,
):
    nx, ny, nz = grid
    ndp = nx * ny * 2
    frames = enc.shape[0]
    rows = frames * KEPT
    width, vlocal = w.shape
    own_rows = pred_hbm.shape[0]
    dp = lax.axis_index("dp")
    z = lax.axis_index("vocab")
    cx = dp // (2 * ny)
    cy = lax.rem(dp // 2, ny)
    core = lax.rem(dp, 2)
    wx = nx - 1
    wy = ny - 1

    def zpeer(i):
        return (dp, lax.rem(z + i, nz))

    def xpeer(i):
        return ((lax.rem(cx + i, nx) * ny + cy) * 2 + core, z)

    def ypeer(i):
        return ((cx * ny + lax.rem(cy + i, ny)) * 2 + core, z)

    partner = (dp + 1 - 2 * core, z)
    following = (lax.rem(dp + 1, ndp), z)
    before = (lax.rem(dp + ndp - 1, ndp), z)

    loads = []
    for i, (src, dst) in enumerate(
        (
            (futt_hbm, futt),
            (pstart_hbm, pstart),
            (labels_hbm, labels),
            (ulen_hbm, ulen),
            (bocc_hbm, bocc),
            (locc_hbm, locc),
            (fw_hbm, fw),
            (enc_hbm, enc),
            (pred_hbm, table.at[pl.ds(own_rows, own_rows)]),
            (w_hbm, w),
        )
    ):
        cp = pltpu.make_async_copy(src, dst, local_sem.at[i])
        cp.start()
        loads.append(cp)

    barrier = pltpu.get_barrier_semaphore()
    peers = [zpeer(i) for i in range(1, nz)] + [xpeer(i) for i in range(1, nx)]
    peers += [ypeer(i) for i in range(1, ny)] + [partner, following, before]
    for peer in peers:
        pl.semaphore_signal(barrier, inc=1, device_id=peer, device_id_type=MESH)

    def remote(src, dst, ssem, rsem, peer):
        return pltpu.make_async_remote_copy(
            src_ref=src, dst_ref=dst, send_sem=ssem, recv_sem=rsem, device_id=peer, device_id_type=MESH
        )

    aux[...] = jnp.zeros_like(aux)
    tail = act32.shape[0] - rows
    act32[pl.ds(rows, tail), :] = jnp.zeros((tail, width), F32)
    gbuf[pl.ds(rows, tail), :] = jnp.zeros((tail, vlocal), BF16)
    picker[pl.ds(rows, tail), :] = jnp.zeros((tail, 2 * own_rows), BF16)
    stat[...] = jnp.zeros_like(stat)
    scol[...] = jnp.zeros_like(scol)
    pl.semaphore_wait(barrier, len(peers))
    pred_copy = remote(
        pred_hbm, table.at[pl.ds(0, own_rows)], pred_sem.at[0], pred_sem.at[1], following
    )
    pred_copy.start()

    for cp in loads[:8]:
        cp.wait()
    aux[0:1, 0:frames] = ((futt[...] - (dp - 1) * (own_rows // 64)) * 64 + pstart[...]).astype(F32)
    aux[1:2, 0:frames] = futt[...].astype(F32)
    aux[2:3, 0:frames] = pstart[...].astype(F32)
    aux[8 : 8 + KEPT, 0:frames] = labels[...].astype(F32)
    aux[16 : 16 + KEPT, 0:frames] = fw[...] * bocc[...]
    aux[24 : 24 + KEPT, 0:frames] = fw[...] * locc[...]
    auxt[...] = aux[...].T

    def column(i):
        return auxt[0:frames, i : i + 1]

    utts = ulen.shape[1]
    futt_col = column(1).astype(jnp.int32)
    found = futt_col == iota((frames, utts), 1)
    limit = jnp.sum(jnp.where(found, ulen[...].astype(F32), 0.0), axis=1, keepdims=True)
    start_col = column(2)
    base_col = column(0).astype(jnp.int32)
    lane = iota((frames, LANES), 1)
    first = jnp.logical_and(lane == 0, z == 0)
    table_iota = iota((frames, 2 * own_rows), 1)
    for k in range(KEPT):
        at = pl.ds(k * frames, frames)
        valid = (start_col + float(k) < limit).astype(F32)
        label_coef = column(24 + k) * valid
        blank_coef = column(16 + k)
        labrep[at, :] = jnp.broadcast_to(column(8 + k).astype(jnp.int32) - z * vlocal, (frames, LANES))
        lrep[at, :] = jnp.broadcast_to(label_coef, (frames, LANES))
        bl0[at, :] = jnp.where(first, jnp.broadcast_to(blank_coef, (frames, LANES)), 0.0)
        coef[at, :] = jnp.broadcast_to(blank_coef + label_coef, (frames, LANES))
        picker[at, :] = (base_col + k == table_iota).astype(BF16)

    loads[8].wait()
    pred_copy.wait()
    for k in range(KEPT):
        at = pl.ds(k * frames, frames)
        picked = jnp.dot(picker[at, :], table[...], preferred_element_type=F32)
        act = jnp.tanh(enc[...].astype(F32) + picked)
        act32[at, :] = act
        actb[at, :] = act.astype(BF16)
    share = width // ndp
    for i in range(act32.shape[0] // LANES):
        cols = pl.ds(i * LANES, LANES)
        turned = act32[cols, :].T
        actt[:, cols] = turned
        split = turned.reshape(nx * ny, 2, share, LANES)
        for c in range(2):
            actp[pl.ds(c * (width // 2), width // 2), cols] = (
                split[:, c].reshape(width // 2, LANES).astype(BF16)
            )

    loads[9].wait()

    stat_copies = []

    def logits_cols(h, cols):
        r0 = h * HALF
        count = min(HALF, rows - r0)
        block = jnp.dot(actb[pl.ds(r0, count), :], w[:, cols], preferred_element_type=F32)
        ebuf[pl.ds(r0, count), cols] = block
        top = mx[h, pl.ds(0, count), :]
        for t in range(block.shape[1] // LANES):
            top = jnp.maximum(top, block[:, t * LANES : (t + 1) * LANES])
        mx[h, pl.ds(0, count), :] = top

    def spread_peak(h):
        count = min(HALF, rows - h * HALF)
        peaks = jnp.max(mx[h, pl.ds(0, count), :], axis=1, keepdims=True)
        mx[h, pl.ds(0, count), :] = jnp.broadcast_to(peaks, (count, LANES))

    def exp_rows(h, first_row, count):
        local = pl.ds(first_row, count)
        at = pl.ds(h * HALF + first_row, count)
        wide = mx[h, local, :]
        total = jnp.zeros((count, LANES), F32)
        for t in range(vlocal // LANES):
            cols = pl.ds(t * LANES, LANES)
            e = jnp.exp(ebuf[at, cols] - wide)
            ebuf[at, cols] = e
            total = total + e
        sums[local, :] = total

    def send_stats(h):
        r0 = h * HALF
        count = min(HALF, rows - r0)
        totals = jnp.sum(sums[pl.ds(0, count), :], axis=1, keepdims=True)
        group = iota((count, LANES), 0) // LANES
        lanes = iota((count, LANES), 1)
        stat[pl.ds(r0, count), :] = jnp.where(
            lanes == group, mx[h, pl.ds(0, count), :], jnp.where(lanes == group + 4, totals, 0.0)
        )
        packed = stat[pl.ds(r0, LANES), :]
        for b in range(1, 4):
            packed = packed + stat[pl.ds(r0 + b * LANES, LANES), :]
        ssend[h] = packed.T[0:8, :]
        copies = []
        for i in range(1, nz):
            cp = remote(
                ssend.at[h], srecv.at[h, i - 1], stat_ssem.at[h, i - 1], stat_rsem.at[h, i - 1], zpeer(i)
            )
            cp.start()
            copies.append(cp)
        stat_copies.append(copies)

    mx[...] = jnp.full(mx.shape, -jnp.inf, F32)

    def logits_step(c, carry):
        logits_cols(0, pl.ds(pl.multiple_of(c * LCOLS, LCOLS), LCOLS))
        return carry

    lax.fori_loop(0, vlocal // LCOLS, logits_step, 0)
    spread_peak(0)
    beside = 2
    for c in range(vlocal // WCOLS):
        logits_cols(1, pl.ds(c * WCOLS, WCOLS))
        if c < beside:
            exp_rows(0, c * (HALF // beside), HALF // beside)
        if c == beside - 1:
            send_stats(0)
    spread_peak(1)

    def exp_step(b, carry):
        exp_rows(1, pl.multiple_of(b * EROWS, EROWS), EROWS)
        return carry

    lax.fori_loop(0, (rows - HALF) // EROWS, exp_step, 0)
    send_stats(1)

    slice_rows = width // nz

    def grad_scale(h):
        r0 = h * HALF
        for cp in stat_copies[h]:
            cp.wait()
        mine = ssend[h]
        peak = mine[0:4]
        for i in range(nz - 1):
            peak = jnp.maximum(peak, srecv[h, i][0:4])
        total = mine[4:8] * jnp.exp(mine[0:4] - peak)
        for i in range(nz - 1):
            got = srecv[h, i]
            total = total + got[4:8] * jnp.exp(got[0:4] - peak)
        scol[0:4, :] = jnp.exp(mine[0:4] - peak) / total
        turned = scol[...].T
        for b in range(4):
            at = pl.ds(r0 + b * LANES, LANES)
            frep[at, :] = jnp.broadcast_to(turned[:, b : b + 1], (LANES, LANES)) * coef[at, :]

    def grad_rows(first_row, count):
        at = pl.ds(first_row, count)
        scale = frep[at, :]
        label = labrep[at, :]
        lcoef = lrep[at, :]
        lanes = iota((count, LANES), 1)
        for t in range(vlocal // LANES):
            cols = pl.ds(t * LANES, LANES)
            value = ebuf[at, cols] * scale - jnp.where(label - t * LANES == lanes, lcoef, 0.0)
            if t == 0:
                value = value - bl0[at, :]
            gbuf[at, cols] = value.astype(BF16)

    h_copies = {}
    relay_copies = {}

    def hidden_cols(h, cols):
        g = gbuf[pl.ds(h * HALF, HALF), cols]
        return lax.dot_general(w[:, cols], g, (((1,), (1,)), ((), ())), preferred_element_type=F32)

    def hidden_send(h):
        hsend[h] = hsum[...].astype(BF16).reshape(nz, slice_rows, HALF)
        copies = []
        quarter = HALF // 2
        plan = [
            (hsend.at[h, lax.rem(z + 4, nz), :, pl.ds(0, quarter)], half_far.at[h, 0], 2),
            (hsend.at[h, lax.rem(z + 4, nz), :, pl.ds(quarter, quarter)], half_far.at[h, 1], nz - 2),
            (hsend.at[h, lax.rem(z + 3, nz)], far.at[h, 0], 1),
            (hsend.at[h, lax.rem(z + nz - 3, nz)], far.at[h, 1], nz - 1),
            (hsend.at[h, lax.rem(z + 1, nz)], near.at[h, 0], 1),
            (hsend.at[h, lax.rem(z + nz - 1, nz)], near.at[h, 1], nz - 1),
        ]
        for n, (src, dst, shift) in enumerate(plan):
            cp = remote(src, dst, h_ssem.at[h, n], h_rsem.at[h, n], zpeer(shift))
            cp.start()
            copies.append(cp)
        h_copies[h] = copies

    def relay_half(h):
        copies = []
        quarter = HALF // 2
        for side, shift in ((0, 2), (1, nz - 2)):
            h_copies[h][side].wait()
            h_copies[h][2 + side].wait()
            own = lax.rem(z + shift, nz)
            for part in range(2):
                cols = pl.ds(part * quarter, quarter)
                total = hsend[h, own, :, cols].astype(F32) + far[h, side, :, cols].astype(F32)
                if part == side:
                    total = total + half_far[h, side].astype(F32)
                rsend[h, side, :, cols] = total.astype(BF16)
            cp = remote(
                rsend.at[h, side],
                relayed.at[h, side],
                h_ssem.at[h, 6 + side],
                h_rsem.at[h, 6 + side],
                zpeer(shift),
            )
            cp.start()
            copies.append(cp)
        relay_copies[h] = copies

    def hidden_finish():
        act_at = pl.ds(pl.multiple_of(z * slice_rows, slice_rows), slice_rows)
        for h in range(2):
            cols = pl.ds(h * HALF, HALF)
            for cp in h_copies[h][4:] + relay_copies[h]:
                cp.wait()
            total = hsend[h, z].astype(F32)
            for i in range(2):
                total = total + near[h, i].astype(F32) + relayed[h, i].astype(F32)
            act = actt[act_at, cols]
            agrad[:, cols] = total * (1.0 - act * act)
        grads = agrad[...]
        summed = grads[:, 0:frames]
        for k in range(1, KEPT):
            summed = summed + grads[:, k * frames : (k + 1) * frames]
        ge_ref[...] = summed
        high = grads.astype(BF16)
        low = (grads - high.astype(F32)).astype(BF16)
        slots = jnp.dot(high, picker[...], preferred_element_type=F32) + jnp.dot(
            low, picker[...], preferred_element_type=F32
        )
        gpsend[...] = slots[:, 0:own_rows]
        gp_copy = remote(gpsend, gprecv, gp_sem.at[0], gp_sem.at[1], before)
        gp_copy.start()
        return slots, gp_copy

    chunks = vlocal // WCOLS
    half_rows = width // 2
    c_copies, p1_copies, p2_copies = {}, {}, {}

    def weight_chunk(c):
        slot = c % 3
        pbuf[slot] = jnp.dot(
            actp[...], gbuf[:, pl.ds(c * WCOLS, WCOLS)], preferred_element_type=F32
        )
        theirs = pl.ds(pl.multiple_of((1 - core) * half_rows, half_rows), half_rows)
        csend[c] = pbuf[slot, theirs, :].astype(BF16)
        cp = remote(csend.at[c], crecv.at[c], c_ssem.at[c], c_rsem.at[c], partner)
        cp.start()
        c_copies[c] = cp

    def weight_first(c):
        c_copies[c].wait()
        mine = pl.ds(pl.multiple_of(core * half_rows, half_rows), half_rows)
        both = pbuf[c % 3, mine, :] + crecv[c].astype(F32)
        both = both.astype(BF16).reshape(nx, ny, share, WCOLS)
        wleft[c] = both[:, :, :, : WCOLS // 2]
        for i in range(ny):
            wright[c, i] = both[:, i, :, WCOLS // 2 :]
        copies = []
        for i in sorted(range(1, nx), key=lambda i: -min(i, nx - i)):
            cp = remote(
                wleft.at[c, lax.rem(cx + i, nx)],
                xr1.at[c, i - 1],
                p1_ssem.at[c, i - 1],
                p1_rsem.at[c, i - 1],
                xpeer(i),
            )
            cp.start()
            copies.append(cp)
        for i in sorted(range(1, ny), key=lambda i: -min(i, ny - i)):
            cp = remote(
                wright.at[c, lax.rem(cy + i, ny)],
                yr1.at[c, i - 1],
                p1_ssem.at[c, wx + i - 1],
                p1_rsem.at[c, wx + i - 1],
                ypeer(i),
            )
            cp.start()
            copies.append(cp)
        p1_copies[c] = copies

    def weight_second(c):
        for cp in p1_copies[c]:
            cp.wait()
        total = wleft[c, cx].astype(F32)
        for i in range(wx):
            total = total + xr1[c, i].astype(F32)
        yst32[c] = total
        yst[c] = total.astype(BF16)
        total = wright[c, cy].astype(F32)
        for i in range(wy):
            total = total + yr1[c, i].astype(F32)
        xst32[c] = total
        xst[c] = total.astype(BF16)
        copies = []
        for i in range(1, ny):
            cp = remote(
                yst.at[c, lax.rem(cy + i, ny)],
                yr2.at[c, i - 1],
                p2_ssem.at[c, i - 1],
                p2_rsem.at[c, i - 1],
                ypeer(i),
            )
            cp.start()
            copies.append(cp)
        for i in range(1, nx):
            cp = remote(
                xst.at[c, lax.rem(cx + i, nx)],
                xr2.at[c, i - 1],
                p2_ssem.at[c, wy + i - 1],
                p2_rsem.at[c, wy + i - 1],
                xpeer(i),
            )
            cp.start()
            copies.append(cp)
        p2_copies[c] = copies

    def weight_last(c):
        for cp in p2_copies[c]:
            cp.wait()
        total = yst32[c, cy]
        for i in range(wy):
            total = total + yr2[c, i].astype(F32)
        gw_ref[:, pl.ds(c * WCOLS, WCOLS // 2)] = total
        total = xst32[c, cx]
        for i in range(wx):
            total = total + xr2[c, i].astype(F32)
        gw_ref[:, pl.ds(c * WCOLS + WCOLS // 2, WCOLS // 2)] = total

    grad_scale(0)

    def grad_step(b, carry):
        grad_rows(pl.multiple_of(b * 64, 64), 64)
        return carry

    lax.fori_loop(0, HALF // 64, grad_step, 0)
    alone = chunks * 2 // 5
    spread = rows - HALF
    part = -(-spread // (chunks - alone) // 16) * 16
    for c in range(chunks):
        if c == alone:
            grad_scale(1)
        value = hidden_cols(0, pl.ds(c * WCOLS, WCOLS))
        hsum[...] = value if c == 0 else hsum[...] + value
        if c >= alone:
            done = (c - alone) * part
            grad_rows(HALF + done, min(part, spread - done))
    hidden_send(0)
    weight_chunk(0)
    weight_chunk(1)
    hsum[...] = hidden_cols(1, pl.ds(0, vlocal))
    hidden_send(1)
    weight_first(0)
    relay_half(0)
    for c in range(2, chunks):
        weight_chunk(c)
        if c >= 3:
            weight_first(c - 2)
    weight_first(chunks - 2)
    weight_second(0)
    weight_first(chunks - 1)
    relay_half(1)
    for c in range(1, chunks - 2):
        weight_second(c)
    slots, gp_copy = hidden_finish()
    weight_second(chunks - 2)
    weight_second(chunks - 1)
    for c in range(chunks):
        weight_last(c)
    gp_copy.wait()
    gp_ref[...] = (slots[:, own_rows:] + gprecv[...]).T


def handover(*refs):
    sems = refs[6]
    copies = [pltpu.make_async_copy(refs[i], refs[3 + i], sems.at[i]) for i in range(3)]
    for cp in copies:
        cp.start()
    for cp in copies:
        cp.wait()


def body(grid, enc, pred, w, futt, pstart, labels, ulen, bocc, locc, fw):
    nx, ny, nz = grid
    frames, width = enc.shape
    vlocal = w.shape[1]
    slots, depth, _ = pred.shape
    own_rows = slots * depth
    rows_pad = 2 * HALF
    share = width // (nx * ny * 2)
    utts = ulen.shape[0]
    chunks = vlocal // WCOLS
    hw = WCOLS // 2
    vm = pltpu.VMEM
    dma = pltpu.SemaphoreType.DMA
    i32 = jnp.int32
    scratch = [
        vm((frames, width), BF16),
        vm((2 * own_rows, width), BF16),
        vm((width, vlocal), BF16),
        vm((1, frames), i32),
        vm((1, frames), i32),
        vm((KEPT, frames), i32),
        vm((1, utts), i32),
        vm((KEPT, frames), F32),
        vm((KEPT, frames), F32),
        vm((1, frames), F32),
        vm((LANES, 2 * LANES), F32),
        vm((2 * LANES, LANES), F32),
        vm((rows_pad, LANES), i32),
        vm((rows_pad, LANES), F32),
        vm((rows_pad, LANES), F32),
        vm((rows_pad, LANES), F32),
        vm((rows_pad, LANES), F32),
        vm((rows_pad, 2 * own_rows), BF16),
        vm((rows_pad, width), F32),
        vm((rows_pad, width), BF16),
        vm((width, rows_pad), F32),
        vm((width, rows_pad), BF16),
        vm((frames * KEPT, vlocal), F32),
        vm((2, HALF, LANES), F32),
        vm((HALF, LANES), F32),
        vm((rows_pad, LANES), F32),
        vm((2, 8, LANES), F32),
        vm((2, nz - 1, 8, LANES), F32),
        vm((LANES, LANES), F32),
        vm((rows_pad, vlocal), BF16),
        vm((width, HALF), F32),
        vm((2, nz, width // nz, HALF), BF16),
        vm((2, 2, width // nz, HALF), BF16),
        vm((2, 2, width // nz, HALF // 2), BF16),
        vm((2, 2, width // nz, HALF), BF16),
        vm((2, 2, width // nz, HALF), BF16),
        vm((2, 2, width // nz, HALF), BF16),
        vm((width // nz, rows_pad), F32),
        vm((3, width, WCOLS), F32),
        vm((chunks, width // 2, WCOLS), BF16),
        vm((chunks, width // 2, WCOLS), BF16),
        vm((chunks, nx, ny, share, hw), BF16),
        vm((chunks, ny, nx, share, hw), BF16),
        vm((chunks, nx - 1, ny, share, hw), BF16),
        vm((chunks, ny, share, hw), BF16),
        vm((chunks, ny, share, hw), F32),
        vm((chunks, ny - 1, share, hw), BF16),
        vm((chunks, ny - 1, nx, share, hw), BF16),
        vm((chunks, nx, share, hw), BF16),
        vm((chunks, nx, share, hw), F32),
        vm((chunks, nx - 1, share, hw), BF16),
        vm((width // nz, own_rows), F32),
        vm((width // nz, own_rows), F32),
        dma((10,)),
        dma((2,)),
        dma((2, nz - 1)),
        dma((2, nz - 1)),
        dma((2, 8)),
        dma((2, 8)),
        dma((chunks,)),
        dma((chunks,)),
        dma((chunks, nx + ny - 2)),
        dma((chunks, nx + ny - 2)),
        dma((chunks, nx + ny - 2)),
        dma((chunks, nx + ny - 2)),
        dma((2,)),
    ]
    results = pl.pallas_call(
        functools.partial(kernel, grid),
        out_shape=(
            jax.ShapeDtypeStruct((share, vlocal), F32),
            jax.ShapeDtypeStruct((width // nz, frames), F32),
            jax.ShapeDtypeStruct((own_rows, width // nz), F32),
        ),
        in_specs=[pl.BlockSpec(memory_space=pl.ANY)] * 10,
        out_specs=[pl.BlockSpec(memory_space=pltpu.VMEM)] * 3,
        scratch_shapes=scratch,
        compiler_params=pltpu.CompilerParams(
            collective_id=0, has_side_effects=True, vmem_limit_bytes=60 * 2**20
        ),
    )(
        enc,
        pred.reshape(own_rows, width),
        w,
        futt.reshape(1, frames),
        pstart.reshape(1, frames),
        labels.T,
        ulen.reshape(1, utts),
        bocc.T,
        locc.T,
        fw.reshape(1, frames),
    )
    gw, ge, gp = pl.pallas_call(
        handover,
        out_shape=tuple(jax.ShapeDtypeStruct(r.shape, r.dtype) for r in results),
        in_specs=[pl.BlockSpec(memory_space=pltpu.VMEM)] * 3,
        out_specs=[pl.BlockSpec(memory_space=pl.ANY)] * 3,
        scratch_shapes=[dma((3,))],
    )(*results)
    return gw, ge.T, gp.reshape(slots, depth, width // nz)


def solution(mesh, sizes=(4, 4)):
    grid = (sizes[0], sizes[1], mesh.shape["vocab"])
    in_specs = (
        P("dp", None),
        P("dp", None, None),
        P(None, "vocab"),
        P("dp"),
        P("dp"),
        P("dp", None),
        P(),
        P("dp", None),
        P("dp", None),
        P("dp"),
    )
    out_specs = (P("dp", "vocab"), P("dp", "vocab"), P("dp", None, "vocab"))
    return jax.shard_map(
        functools.partial(body, grid), mesh=mesh, in_specs=in_specs, out_specs=out_specs, check_vma=False
    )
```
